128 devices in a mesh: station: 32 (over z, y_hi, x), tm: 4 (over y_lo, core).
Axes of the slice: x: 4, y: 4 (y_hi: 2, y_lo: 2; y = y_hi * 2 + y_lo), z: 4, core: 2. Of those that a mesh axis runs over, the one named last changes fastest.
Arguments:
- spectra: bfloat16 [4, 48, 2048, 1024], P('tm', None, 'station'), may hold values from -80 to 80
- counts: int32 [4, 2048], P('tm', 'station'), may hold values from 1 to 48, as said below
- block_ids: int32 [2], replicated, may hold values from 0 to 31
Outputs:
- correlations: bfloat16 [2, 64, 2048, 512], P(None, 'tm', 'station')
The draws below stay inside these ranges and needn't reach their ends.
Inputs may be any that keep to these rules, and one draw needn't show every extreme that they name: Subwindow s of channel c in window w is live when s < counts[w, c]; later subwindows are gaps. `block_ids`: block b holds channels b * 64 to (b + 1) * 64 - 1.
All inputs are finite; a program needn't handle non-finite values.
Results may differ from the reference program's by a relative error of at most 0.0056.
Values may be sent and summed in bfloat16 or wider, within the bound.
No kernel may reach another device: no remote copies, remote signals or barrier semaphores. Data moves between devices by JAX's collectives and lax.ppermute only.
A program may use at most 320 MiB of HBM per device.

```python
import math
import jax
import jax.numpy as jnp
from jax import lax

NFFT = 2048
BINS = 512
LAGS = 512
BLOCK = 64
STEPS = 2
CHAN_DEV = 64
SUBWIN = 48
WINDOWS = 4
CHANNELS = 2048
NBLOCKS = 32
N_STATION = 32


def draw_counts(key, part):
    key = jax.random.fold_in(key, 11)
    keys_all = jax.random.split(key, 2)
    full_flag = jax.random.randint(keys_all[0], (WINDOWS, CHANNELS), 0, 10) < 7
    spread_count = jax.random.randint(keys_all[1], (WINDOWS, CHANNELS), 1, SUBWIN + 1)
    return jnp.where(full_flag, SUBWIN, spread_count).astype(jnp.int32)


def draw_spectra(key, part):
    key = jax.random.fold_in(key, 7)
    keys_all = jax.random.split(key, 6)
    shape_full = (WINDOWS, SUBWIN, CHANNELS, 2 * BINS)
    row_scale = jnp.exp(jax.random.uniform(keys_all[1], (WINDOWS, SUBWIN, CHANNELS, 1), jnp.float32, 0.0, math.log(10.0)))
    dropped_flag = jax.random.randint(keys_all[4], (WINDOWS, 1, CHANNELS), 0, 10) < 3
    dropped_from = jax.random.randint(keys_all[5], (WINDOWS, 1, CHANNELS), 0, SUBWIN)
    cut_row = jnp.where(dropped_flag, dropped_from, SUBWIN)
    subwin_pos = lax.broadcasted_iota(jnp.int32, (WINDOWS, SUBWIN, CHANNELS), 1)
    kept_rows = (subwin_pos < cut_row).astype(jnp.float32)[..., None]
    noise_draw = jnp.clip(jax.random.normal(keys_all[0], shape_full, jnp.float32), -4.0, 4.0)
    return (noise_draw * row_scale * kept_rows).astype(jnp.bfloat16)


def setup_inputs(seed: int = 0) -> dict:
    streams_of = jax.random.split(jax.random.key(seed), 4)
    spectra = draw_spectra(jax.random.fold_in(streams_of[3], 71), 0)
    counts = draw_counts(jax.random.fold_in(streams_of[3], 71), 0)
    block_ids = jax.random.randint(streams_of[2], (STEPS,), 0, NBLOCKS).astype(jnp.int32)
    return {"spectra": spectra, "counts": counts, "block_ids": block_ids}


eps_value = 1e-06

def whiten(spectra, counts):
    values = spectra.astype(jnp.float32)
    mean_power = lax.optimization_barrier(jnp.mean(values * values, axis=-1, keepdims=True))
    subwin_pos = lax.broadcasted_iota(jnp.int32, (counts.shape[0], SUBWIN, counts.shape[1]), 1)
    valid_mask = (subwin_pos < counts[:, None, :]).astype(jnp.float32)
    return (values * lax.rsqrt(mean_power + eps_value) * valid_mask[..., None]).astype(jnp.bfloat16)

def window_corr(source, source_counts, receiver, receiver_counts):
    src_vals = source.astype(jnp.float32)
    rec_vals = receiver.astype(jnp.float32)
    src_real = src_vals[..., :BINS]
    src_imag = src_vals[..., BINS:]
    rec_real = rec_vals[..., :BINS]
    rec_imag = rec_vals[..., BINS:]
    real_part = jnp.einsum('sjk,srk->jrk', src_real, rec_real) + jnp.einsum('sjk,srk->jrk', src_imag, rec_imag)
    imag_part = jnp.einsum('sjk,srk->jrk', src_real, rec_imag) - jnp.einsum('sjk,srk->jrk', src_imag, rec_real)
    pair_count = jnp.minimum(source_counts[:, None], receiver_counts[None, :]).astype(jnp.float32)
    real_part = real_part / pair_count[..., None]
    imag_part = imag_part / pair_count[..., None]
    spectrum = lax.complex(real_part, imag_part)
    padded = jnp.pad(spectrum, ((0, 0), (0, 0), (1, NFFT // 2 - BINS)))
    signal = jnp.fft.irfft(padded, n=NFFT, axis=-1) * (NFFT / (2.0 * math.sqrt(BINS)))
    return jnp.concatenate([signal[..., NFFT - LAGS // 2:], signal[..., :LAGS // 2]], axis=-1).astype(jnp.float32)

def reference(spectra, counts, block_ids):
    normed = whiten(spectra, counts)
    results = []
    for position in range(STEPS):
        first_channel = (block_ids[position] * BLOCK).astype(jnp.int32)
        source = lax.dynamic_slice_in_dim(normed, first_channel, BLOCK, 2)
        source_counts = lax.dynamic_slice_in_dim(counts, first_channel, BLOCK, 1)

        def shard_corr(shard_index):
            begin_channel = (shard_index * CHAN_DEV).astype(jnp.int32)
            receiver = lax.dynamic_slice_in_dim(normed, begin_channel, CHAN_DEV, 2)
            receiver_counts = lax.dynamic_slice_in_dim(counts, begin_channel, CHAN_DEV, 1)
            running = jnp.zeros((BLOCK, CHAN_DEV, LAGS), jnp.float32)
            for window in range(WINDOWS):
                running = running + window_corr(source[window], source_counts[window], receiver[window], receiver_counts[window])
            return running.astype(jnp.bfloat16)
        pieces = lax.map(shard_corr, jnp.arange(N_STATION, dtype=jnp.int32))
        results.append(jnp.transpose(pieces, (1, 0, 2, 3)).reshape(BLOCK, CHANNELS, LAGS))
    return jnp.stack(results)
```

```python
import functools, math
import jax
import jax.numpy as jnp
import numpy as np
from jax import lax
from jax.experimental import pallas as pl
from jax.experimental.pallas import tpu as pltpu

NFFT, BINS, LAGS, BLOCK, STEPS, SUB = 2048, 512, 512, 64, 2, 48
EPS = 1e-6
F32, BF = jnp.float32, jnp.bfloat16
VMEM = pltpu.CompilerParams(vmem_limit_bytes=56 * 2**20)
SB = 16


def whiten_kernel(spec, counts, own, rot, work):
    base = pl.program_id(0) * SB
    live = counts[...]

    def one(s, _):
        v = spec[s].astype(F32)
        power = jnp.mean(v * v, axis=-1, keepdims=True)
        mask = (base + s < live).astype(F32)
        n = v * lax.rsqrt(power + EPS) * mask
        m = jnp.concatenate([n[:, :BINS], n[:, BINS:]], axis=0)
        work[:, s, :] = m.T
        return 0

    for s in range(SB):
        one(s, 0)
    whole = work[...]
    own[...] = whole.astype(BF)
    lane = lax.broadcasted_iota(jnp.int32, (1, 1, 128), 2)
    turned = pltpu.roll(whole, 64, 2)
    rot[...] = jnp.where(lane < 64, turned, -turned).astype(BF)


def whiten(spectra, counts):
    return pl.pallas_call(
        whiten_kernel,
        grid=(SUB // SB,),
        in_specs=[
            pl.BlockSpec((SB, BLOCK, 2 * BINS), lambda i: (i, 0, 0)),
            pl.BlockSpec((BLOCK, 1), lambda i: (0, 0)),
        ],
        out_specs=[pl.BlockSpec((BINS, SB, 128), lambda i: (0, i, 0))] * 2,
        out_shape=[jax.ShapeDtypeStruct((BINS, SUB, 128), BF)] * 2,
        scratch_shapes=[pltpu.VMEM((BINS, SB, 128), F32)],
        compiler_params=VMEM,
        name="whiten",
    )(spectra, counts[:, None])


KC = 32


def corr_kernel(src, own, rot, inv, table, out, cross, rows):
    step = pl.program_id(0)
    for k in range(KC):
        x = src[k].T
        h = jnp.dot(x[:BLOCK], own[k], preferred_element_type=F32)
        h += jnp.dot(x[BLOCK:], rot[k], preferred_element_type=F32)
        cross[k] = h
    for j in range(BLOCK):
        rows[j, pl.ds(pl.multiple_of(step * KC, KC), KC), :] = cross[:, j, :].astype(BF)

    @pl.when(step == BINS // KC - 1)
    def _():
        def quad(q, _):
            a = [rows[4 * q + i] for i in range(4)]
            rhs = jnp.concatenate(
                [
                    jnp.concatenate([v[:, :BLOCK] for v in a], axis=1),
                    jnp.concatenate([v[:, BLOCK:] for v in a], axis=1),
                ],
                axis=0,
            )
            y = jnp.dot(table[...], rhs, preferred_element_type=F32)
            col = pl.multiple_of((q % 4) * 256, 256)
            out[q // 4, :, pl.ds(col, 256)] = (y * inv[q // 4, :, pl.ds(col, 256)]).astype(BF)
            return 0

        lax.fori_loop(0, BLOCK // 4, quad, 0)


def corr(src, own, rot, inv, table):
    blk = pl.BlockSpec((KC, SUB, 128), lambda i: (i, 0, 0))
    return pl.pallas_call(
        corr_kernel,
        grid=(BINS // KC,),
        in_specs=[
            blk,
            blk,
            blk,
            pl.BlockSpec((4, 1, 1024), lambda i: (0, 0, 0)),
            pl.BlockSpec((LAGS, 2 * BINS), lambda i: (0, 0)),
        ],
        out_specs=pl.BlockSpec((4, LAGS, 1024), lambda i: (0, 0, 0)),
        out_shape=jax.ShapeDtypeStruct((4, LAGS, 1024), BF),
        scratch_shapes=[
            pltpu.VMEM((KC, BLOCK, 128), F32),
            pltpu.VMEM((BLOCK, BINS, 128), BF),
        ],
        compiler_params=VMEM,
        name="corr",
    )(src, own, rot, inv, table)


def finish_kernel(a, b, out):
    out[0] = (a[0].astype(F32) + b[0].astype(F32)).T.astype(BF)


def finish(a, b):
    n = a.shape[0]
    blk = pl.BlockSpec((1, LAGS, 256), lambda i, j: (i, 0, j))
    return pl.pallas_call(
        finish_kernel,
        grid=(n, 4),
        in_specs=[blk, blk],
        out_specs=pl.BlockSpec((1, 256, LAGS), lambda i, j: (i, j, 0)),
        out_shape=jax.ShapeDtypeStruct((n, 1024, LAGS), BF),
        compiler_params=VMEM,
        name="finish",
    )(a, b)


def lag_table():
    k = np.arange(1, BINS + 1)[None, :]
    tau = np.arange(LAGS)[:, None] - LAGS // 2
    ph = ((k * tau) % NFFT) * (2 * np.pi / NFFT)
    w = np.concatenate([np.cos(ph), -np.sin(ph)], axis=1) / math.sqrt(BINS)
    return jnp.asarray(w, BF)


def pair_sum(lag):
    tm = lax.axis_index("tm")
    low, core = tm // 2, tm % 2
    lag = lag.reshape(2, 2, LAGS, 1024)
    away = lax.dynamic_index_in_dim(lag, 1 - core, 1, keepdims=False)
    keep = lax.dynamic_index_in_dim(lag, core, 1, keepdims=False)
    got = lax.ppermute(away, "tm", [(t, t ^ 1) for t in range(4)])
    both = (keep.astype(F32) + got.astype(F32)).astype(BF)
    away = lax.dynamic_index_in_dim(both, 1 - low, 0, keepdims=False)
    keep = lax.dynamic_index_in_dim(both, low, 0, keepdims=False)
    got = lax.ppermute(away, "tm", [(t, t ^ 2) for t in range(4)])
    return keep, got


def body(spectra, counts, block_ids):
    counts = counts[0]
    table = lag_table()
    all_counts = lax.all_gather(counts, "station")
    own, rot = whiten(spectra[0], counts)
    pieces = lax.all_to_all(own.reshape(32, 16, SUB, 128), "station", 0, 0)
    parts = []
    for i in range(STEPS):
        block = block_ids[i]
        piece = lax.dynamic_index_in_dim(pieces, block, 0, keepdims=False)
        src = lax.all_gather(piece, "station").reshape(BINS, SUB, 128)
        src_counts = lax.dynamic_index_in_dim(all_counts, block, 0, keepdims=False)
        inv = 1.0 / jnp.minimum(src_counts[:, None], counts[None, :]).astype(F32)
        lag = corr(src, own, rot, inv.reshape(4, 1, 1024), table)
        parts.append(pair_sum(lag))
    keep = jnp.stack([p[0] for p in parts])
    got = jnp.stack([p[1] for p in parts])
    return finish(keep, got).reshape(STEPS, 16, BLOCK, LAGS)


def solution(mesh):
    from jax.sharding import PartitionSpec as P

    return jax.shard_map(
        body,
        mesh=mesh,
        in_specs=(P("tm", None, "station", None), P("tm", "station"), P()),
        out_specs=P(None, "tm", "station", None),
        check_vma=False,
    )
```

```python
import math

import jax
import jax.numpy as jnp
import numpy as np
from jax import lax
from jax.experimental import pallas as pl
from jax.experimental.pallas import tpu as pltpu

NFFT, BINS, LAGS, BLOCK, STEPS, SUB = 2048, 512, 512, 64, 2, 48
EPS = 1e-6
F32, BF = jnp.float32, jnp.bfloat16
VMEM = pltpu.CompilerParams(vmem_limit_bytes=56 * 2**20)
SB = 16
KC = 64
CHUNKS = BINS // KC
HALF = BINS // 2


def whiten_kernel(spec, counts, own, work):
    base = pl.program_id(0) * SB
    live = counts[...]
    for s in range(SB):
        v = spec[s].astype(F32)
        power = jnp.mean(v * v, axis=-1, keepdims=True)
        mask = (base + s < live).astype(F32)
        n = v * lax.rsqrt(power + EPS) * mask
        work[s] = jnp.concatenate([n[:, :BINS], n[:, BINS:]], axis=0).T
    own[...] = jnp.swapaxes(work[...], 0, 1).astype(BF)


def whiten(spectra, counts):
    return pl.pallas_call(
        whiten_kernel,
        grid=(SUB // SB,),
        in_specs=[
            pl.BlockSpec((SB, BLOCK, 2 * BINS), lambda i: (i, 0, 0)),
            pl.BlockSpec((BLOCK, 1), lambda i: (0, 0)),
        ],
        out_specs=pl.BlockSpec((BINS, SB, 128), lambda i: (0, i, 0)),
        out_shape=jax.ShapeDtypeStruct((BINS, SUB, 128), BF),
        scratch_shapes=[pltpu.VMEM((SB, BINS, 128), F32)],
        compiler_params=VMEM,
        cost_estimate=pl.CostEstimate(flops=10**8, bytes_accessed=13 * 10**6, transcendentals=0),
        name="whiten",
    )(spectra, counts[:, None])


def turn_kernel(own, rot):
    v = own[...]
    rot[...] = jnp.concatenate([v[..., BLOCK:], -v[..., :BLOCK]], axis=-1)


def turn(own):
    blk = pl.BlockSpec((KC, SUB, 128), lambda i: (i, 0, 0))
    return pl.pallas_call(
        turn_kernel,
        grid=(CHUNKS,),
        in_specs=[blk],
        out_specs=blk,
        out_shape=jax.ShapeDtypeStruct((BINS, SUB, 128), BF),
        compiler_params=VMEM,
        cost_estimate=pl.CostEstimate(flops=10**6, bytes_accessed=25 * 10**6, transcendentals=0),
        name="turn",
    )(own)


def cross_kernel(n, *refs):
    place = refs[0]
    pieces = refs[1 : 1 + n]
    own, rot = refs[1 + n : 3 + n]
    out, src, work, sems = refs[-4:]
    step = pl.program_id(0)
    copies = []
    for m, piece in enumerate(pieces):
        copies.append(pltpu.make_async_copy(piece, src.at[m], sems.at[m]))

    @pl.when(step == 0)
    def _():
        for copy in copies:
            copy.start()

    for m, copy in enumerate(copies):
        @pl.when(step == m)
        def _(copy=copy):
            copy.wait()

    for k in range(KC):
        x = src[step, k].T
        h = jnp.dot(x[:BLOCK], own[k], preferred_element_type=F32)
        h += jnp.dot(x[BLOCK:], rot[k], preferred_element_type=F32)
        work[k] = h
    z = jnp.swapaxes(work[...], 0, 1)
    low = lax.broadcasted_iota(jnp.int32, (KC, 128), 1) < BLOCK
    for p in range(BLOCK // 2):
        u, v = z[2 * p], z[2 * p + 1]
        lanes = slice(p % 2 * 128, p % 2 * 128 + 128)
        out[p // 2, 0, :, lanes] = jnp.where(low, u, pltpu.roll(v, 64, 1)).astype(BF)
        out[p // 2, 1, :, lanes] = jnp.where(low, pltpu.roll(u, 64, 1), v).astype(BF)


def cross(place, pieces, own, rot, base=None):
    n = len(pieces)
    here = pl.BlockSpec((KC, SUB, 128), lambda i, p: (p[i], 0, 0))
    anywhere = pl.BlockSpec(memory_space=pl.ANY)
    extra = [] if base is None else [base]
    return pl.pallas_call(
        lambda *refs: cross_kernel(n, *refs),
        grid_spec=pltpu.PrefetchScalarGridSpec(
            num_scalar_prefetch=1,
            grid=(n,),
            in_specs=[anywhere] * n + [here, here] + [anywhere] * len(extra),
            out_specs=pl.BlockSpec((BLOCK // 4, 2, KC, 256), lambda i, p: (0, 0, p[i], 0)),
            scratch_shapes=[
                pltpu.VMEM((n, KC, SUB, 128), BF),
                pltpu.VMEM((KC, BLOCK, 128), F32),
                pltpu.SemaphoreType.DMA((n,)),
            ],
        ),
        out_shape=jax.ShapeDtypeStruct((BLOCK // 4, 2, BINS, 256), BF),
        input_output_aliases={n + 3: 0} if extra else {},
        compiler_params=VMEM,
        cost_estimate=pl.CostEstimate(
            flops=n * 16 * 10**8, bytes_accessed=n * 4 * 10**6, transcendentals=0
        ),
        name="cross",
    )(place, *pieces, own, rot, *extra)


def lags_kernel(order, rows, inv, table, out):
    for q in range(4):
        y = jnp.dot(table[...], rows[q].reshape(2 * BINS, 256), preferred_element_type=F32)
        cols = slice(q * 256, q * 256 + 256)
        out[0, :, cols] = (y * inv[0, :, cols]).astype(BF)


def lags(order, rows, inv, table):
    n = order.shape[0]
    return pl.pallas_call(
        lags_kernel,
        grid_spec=pltpu.PrefetchScalarGridSpec(
            num_scalar_prefetch=1,
            grid=(n,),
            in_specs=[
                pl.BlockSpec((4, 2, BINS, 256), lambda i, o: (o[i], 0, 0, 0)),
                pl.BlockSpec((1, 1, 1024), lambda i, o: (o[i], 0, 0)),
                pl.BlockSpec((LAGS, 2 * BINS), lambda i, o: (0, 0)),
            ],
            out_specs=pl.BlockSpec((1, LAGS, 1024), lambda i, o: (i, 0, 0)),
        ),
        out_shape=jax.ShapeDtypeStruct((n, LAGS, 1024), BF),
        compiler_params=VMEM,
        cost_estimate=pl.CostEstimate(
            flops=n * 22 * 10**8, bytes_accessed=n * 3 * 10**6, transcendentals=0
        ),
        name="lags",
    )(order, rows, inv, table)


def finish_kernel(a, b, c, *refs):
    total = a[0].astype(F32) + b[0].astype(F32) + c[...].astype(F32)
    refs[-1][0] = total.T.astype(BF)


def finish(step, near, near_got, far_got, base=None):
    cols = 512
    extra = [] if base is None else [base]
    return pl.pallas_call(
        finish_kernel,
        grid=(1024 // cols,),
        in_specs=[
            pl.BlockSpec((1, LAGS, cols), lambda j: (1, 0, j)),
            pl.BlockSpec((1, LAGS, cols), lambda j: (0, 0, j)),
            pl.BlockSpec((LAGS, cols), lambda j: (0, j)),
        ]
        + [pl.BlockSpec(memory_space=pl.ANY)] * len(extra),
        out_specs=pl.BlockSpec((1, cols, LAGS), lambda j: (step, j, 0)),
        out_shape=jax.ShapeDtypeStruct((STEPS, 1024, LAGS), BF),
        input_output_aliases={3: 0} if extra else {},
        compiler_params=VMEM,
        name="finish",
    )(near, near_got, far_got, *extra)


def lag_table():
    k = np.arange(1, BINS + 1)[None, :]
    tau = np.arange(LAGS)[:, None] - LAGS // 2
    ph = ((k * tau) % NFFT) * (2 * np.pi / NFFT)
    w = np.concatenate([np.cos(ph), -np.sin(ph)], axis=1) / math.sqrt(BINS)
    return jnp.asarray(w, BF)


def along_x(a, d):
    return lax.ppermute(a, "station", [(s, s - s % 4 + (s + d) % 4) for s in range(32)])


def along_z(a, d):
    return lax.ppermute(a, "station", [(s, (s + 8 * d) % 32) for s in range(32)])


def swap_y(a):
    return lax.ppermute(a, "station", [(s, s ^ 4) for s in range(32)])


def cut(a, index, size):
    return lax.dynamic_slice_in_dim(a, index * size, size, 0)


def pick(which, options):
    out = options[0]
    for n in range(1, 4):
        out = jnp.where(which == n, options[n], out)
    return out


def barrier(*arrays):
    return lax.optimization_barrier(arrays)


def spread(sends, shifts, work=None, args=()):
    n = len(sends)
    held = barrier(*sends, *args)
    got = [shift(a) for a, shift in zip(held[:n], shifts)]
    done = list(work(*held[n:])) if work else []
    return barrier(*got, *done)


HOPS = (1, 2, 3)
TO_X = [lambda a, d=d: along_x(a, d) for d in HOPS]
TO_Z = [lambda a, d=d: along_z(a, d) for d in HOPS]


def gather_counts(marks):
    for shift in (TO_X[1], TO_Z[0], TO_Z[1], swap_y):
        marks = jnp.stack([marks, shift(marks)])
    return [marks]


def broadcast(own, marks, roots, z, h, x):
    got = spread(
        [cut(own, (x + d) & 3, 64) for d in HOPS]
        + [cut(own, 4 + ((z + d) & 3), 64) for d in HOPS],
        TO_X + TO_Z,
    )
    got_a = [cut(own, x, 64), *got[:3]]
    got_b = [cut(own, 4 + z, 64), *got[3:6]]
    sel_a = [pick((x - r[2]) & 3, got_a) for r in roots]
    sel_b = [pick((z - r[0]) & 3, got_b) for r in roots]

    def some(sel, q):
        return jnp.stack([cut(a, q, 16) for a in sel])

    got = spread(
        [some(sel_a, (z + d) & 3) for d in HOPS]
        + [some(sel_b, (x + d) & 3) for d in HOPS],
        TO_Z + TO_X,
    )
    got_a = [some(sel_a, z), *got[:3]]
    got_b = [some(sel_b, x), *got[3:6]]
    mine = jnp.stack(
        [
            jnp.stack([pick((z - r[0]) & 3, [g[i] for g in got_a]) for i, r in enumerate(roots)]),
            jnp.stack([pick((x - r[2]) & 3, [g[i] for g in got_b]) for i, r in enumerate(roots)]),
        ]
    )
    other, marks = spread([mine], [swap_y], gather_counts, [marks])
    sub = [
        jnp.stack([jnp.where(h == r[1], mine[n, i], other[n, i]) for i, r in enumerate(roots)])
        for n in range(2)
    ]
    got = spread([sub[0]] * 3 + [sub[1]] * 3, TO_Z + TO_X)
    all_a = [sub[0], *got[:3]]
    all_b = [sub[1], *got[3:6]]
    out = []
    for i in range(STEPS):
        a = jnp.concatenate([pick((z - q) & 3, [v[i] for v in all_a]) for q in range(4)])
        b = jnp.concatenate([pick((x - q) & 3, [v[i] for v in all_b]) for q in range(4)])
        out.append((a, b))
    return out, marks


def other_core(a):
    return lax.ppermute(a, "tm", [(t, t ^ 1) for t in range(4)])


def other_chip(a):
    return lax.ppermute(a, "tm", [(t, t ^ 2) for t in range(4)])


def add(a, b):
    return (a.astype(F32) + b.astype(F32)).astype(BF)


def body(spectra, counts, block_ids):
    counts = counts[0]
    table = lag_table()
    station, tm = lax.axis_index("station"), lax.axis_index("tm")
    z, h, x = station >> 3, station >> 2 & 1, station & 3
    next_counts, own = spread([counts], [TO_X[0]], lambda *a: [whiten(*a)], [spectra[0], counts])
    marks = jnp.stack([counts, next_counts])
    roots = [(block_ids[i] >> 3, block_ids[i] >> 2 & 1, block_ids[i] & 3) for i in range(STEPS)]
    starts, marks = broadcast(own, marks, roots, z, h, x)

    def places(*list_of):
        return jnp.stack(list_of).astype(jnp.int32)

    near_by = places(x, (x + 3) & 3, (x + 1) & 3, 4 + z, 4 + ((z + 3) & 3), 4 + ((z + 1) & 3))
    opposite = places((x + 2) & 3, 4 + ((z + 2) & 3))
    everywhere = jnp.concatenate([near_by, opposite])
    far_blocks = places((tm ^ 2) ^ 1, tm ^ 2)
    near_blocks = places(tm ^ 1, tm)

    def scales(marks):
        out = []
        for r in roots:
            dz, dx = (z - r[0]) & 3, (x - r[2]) & 3
            src_counts = marks[h ^ r[1], dz >> 1, dz & 1, dx >> 1, dx & 1]
            inv = 1.0 / jnp.minimum(src_counts[:, None], counts[None, :]).astype(F32)
            out.append(inv.reshape(4, 1, 1024))
        return out

    def far(i, rows):
        return lags(far_blocks, rows, invs[i], table)

    def near(i, rows):
        return lags(near_blocks, rows, invs[i], table)

    (a0, b0), (a1, b1) = starts
    up, down = [TO_X[0], TO_Z[0]], [TO_X[2], TO_Z[2]]
    a0_up, b0_up, a0_down, b0_down, rot, *invs = spread(
        [a0, b0, a0, b0], up + down, lambda v, m: [turn(v), *scales(m)], [own, marks]
    )
    a0_far, b0_far, a1_down, b1_down, rows = spread(
        [a0_up, b0_up, a1, b1],
        up + down,
        lambda *v: [cross(near_by, v[:6], *v[6:])],
        [a0, a0_up, a0_down, b0, b0_up, b0_down, own, rot],
    )

    def work(rows, *v):
        rows = cross(opposite, v[:2], *v[2:], rows)
        return [far(0, rows), near(0, rows)]

    a1_up, b1_up, a1_far, b1_far, far0, near0 = spread(
        [a1, b1, a1_down, b1_down], up + down, work, [rows, a0_far, b0_far, own, rot]
    )
    far_got0, near_got0 = spread([far0[:1], near0[:1]], [other_core] * 2)
    sum0 = add(far0[1], far_got0[0])

    def work(*v):
        rows = cross(everywhere, v[:8], *v[8:])
        return [rows, far(1, rows)]

    far_sum0, rows, far1 = spread(
        [sum0],
        [other_chip],
        work,
        [a1, a1_up, a1_down, b1, b1_up, b1_down, a1_far, b1_far, own, rot],
    )
    (far_got1,) = spread([far1[:1]], [other_core])
    sum1 = add(far1[1], far_got1[0])

    def work(rows, *step0):
        return [near(1, rows), finish(0, *step0)]

    far_sum1, near1, out = spread(
        [sum1], [other_chip], work, [rows, near0, near_got0, far_sum0]
    )
    near_got1 = other_core(near1[:1])
    out = finish(1, near1, near_got1, far_sum1, out)
    return out.reshape(STEPS, 16, BLOCK, LAGS)


def solution(mesh):
    from jax.sharding import PartitionSpec as P

    return jax.shard_map(
        body,
        mesh=mesh,
        in_specs=(P("tm", None, "station", None), P("tm", "station"), P()),
        out_specs=P(None, "tm", "station", None),
        check_vma=False,
    )
```

```python
import math

import jax
import jax.numpy as jnp
import numpy as np
from jax import lax
from jax.experimental import pallas as pl
from jax.experimental.pallas import tpu as pltpu

NFFT, BINS, LAGS, BLOCK, STEPS, SUB = 2048, 512, 512, 64, 2, 48
EPS = 1e-6
F32, BF = jnp.float32, jnp.bfloat16
VMEM = pltpu.CompilerParams(vmem_limit_bytes=56 * 2**20)
SB = 16
KC = 64
CHUNKS = BINS // KC
HALF = BINS // 2


def whiten_kernel(place, spec, counts, *refs):
    own, pieces, work = refs[0], refs[1:-1], refs[-1]
    base = pl.program_id(0) * SB
    live = counts[...]
    for s in range(SB):
        v = spec[s].astype(F32)
        power = jnp.mean(v * v, axis=-1, keepdims=True)
        mask = (base + s < live).astype(F32)
        n = v * lax.rsqrt(power + EPS) * mask
        work[s] = jnp.concatenate([n[:, :BINS], n[:, BINS:]], axis=0).T
    own[...] = jnp.swapaxes(work[...], 0, 1).astype(BF)
    for m, piece in enumerate(pieces):
        piece[...] = own[pl.ds(pl.multiple_of(place[m] * KC, KC), KC)]


def whiten(place, spectra, counts):
    n = place.shape[0]
    return pl.pallas_call(
        whiten_kernel,
        grid_spec=pltpu.PrefetchScalarGridSpec(
            num_scalar_prefetch=1,
            grid=(SUB // SB,),
            in_specs=[
                pl.BlockSpec((SB, BLOCK, 2 * BINS), lambda i, p: (i, 0, 0)),
                pl.BlockSpec((BLOCK, 1), lambda i, p: (0, 0)),
            ],
            out_specs=[pl.BlockSpec((BINS, SB, 128), lambda i, p: (0, i, 0))]
            + [pl.BlockSpec((KC, SB, 128), lambda i, p: (0, i, 0))] * n,
            scratch_shapes=[pltpu.VMEM((SB, BINS, 128), F32)],
        ),
        out_shape=[jax.ShapeDtypeStruct((BINS, SUB, 128), BF)]
        + [jax.ShapeDtypeStruct((KC, SUB, 128), BF)] * n,
        compiler_params=VMEM,
        cost_estimate=pl.CostEstimate(flops=10**8, bytes_accessed=18 * 10**6, transcendentals=0),
        name="whiten",
    )(place, spectra, counts[:, None])


def choose(scalars, inputs, shapes, tasks):
    n = len(inputs)

    def kernel(*refs):
        s, ins, outs, sems = refs[0], refs[1 : 1 + n], refs[1 + n : -1], refs[-1]
        copies = []
        for m, (dst, which, sources) in enumerate(tasks):
            options = [pltpu.make_async_copy(src(ins, s), dst(outs), sems.at[m]) for src in sources]
            for number, copy in enumerate(options):
                @pl.when(s[which] == number)
                def _(copy=copy):
                    copy.start()
            copies.append(options[0])
        for copy in copies:
            copy.wait()

    anywhere = pl.BlockSpec(memory_space=pl.ANY)
    return pl.pallas_call(
        kernel,
        grid_spec=pltpu.PrefetchScalarGridSpec(
            num_scalar_prefetch=1,
            grid=(1,),
            in_specs=[anywhere] * n,
            out_specs=[pl.BlockSpec(shape, lambda i, s, n=len(shape): (0,) * n) for shape in shapes],
            scratch_shapes=[pltpu.SemaphoreType.DMA((len(tasks),))],
        ),
        out_shape=[jax.ShapeDtypeStruct(shape, BF) for shape in shapes],
        compiler_params=VMEM,
        cost_estimate=pl.CostEstimate(flops=10**6, bytes_accessed=6 * 10**6, transcendentals=0),
        name="choose",
    )(scalars, *inputs)


def turn_kernel(own, rot):
    v = own[...]
    rot[...] = jnp.concatenate([v[..., BLOCK:], -v[..., :BLOCK]], axis=-1)


def turn(own):
    blk = pl.BlockSpec((KC, SUB, 128), lambda i: (i, 0, 0))
    return pl.pallas_call(
        turn_kernel,
        grid=(CHUNKS,),
        in_specs=[blk],
        out_specs=blk,
        out_shape=jax.ShapeDtypeStruct((BINS, SUB, 128), BF),
        compiler_params=VMEM,
        cost_estimate=pl.CostEstimate(flops=10**6, bytes_accessed=25 * 10**6, transcendentals=0),
        name="turn",
    )(own)


def corr_kernel(place, order, *refs):
    pieces = refs[:CHUNKS]
    own, rot, inv, table = refs[CHUNKS : CHUNKS + 4]
    outs = refs[CHUNKS + 4 : CHUNKS + 8]
    src, work, rows, sems = refs[CHUNKS + 8 :]
    step = pl.program_id(0)
    copies = [pltpu.make_async_copy(piece, src.at[m], sems.at[m]) for m, piece in enumerate(pieces)]

    @pl.when(step == 0)
    def _():
        for copy in copies:
            copy.start()

    for m, copy in enumerate(copies):
        @pl.when(step == m)
        def _(copy=copy):
            copy.wait()

    for k in range(KC):
        x = src[step, k].T
        h = jnp.dot(x[:BLOCK], own[k], preferred_element_type=F32)
        h += jnp.dot(x[BLOCK:], rot[k], preferred_element_type=F32)
        work[k] = h
    z = jnp.swapaxes(work[...], 0, 1)
    off = pl.multiple_of(place[step] * KC, KC)
    low = lax.broadcasted_iota(jnp.int32, (KC, 128), 1) < BLOCK
    for p in range(BLOCK // 2):
        u, v = z[2 * p], z[2 * p + 1]
        lanes = slice(p % 2 * 128, p % 2 * 128 + 128)
        rows[p // 2, pl.ds(off, KC), lanes] = jnp.where(low, u, pltpu.roll(v, 64, 1)).astype(BF)
        rows[p // 2, pl.ds(off + BINS, KC), lanes] = jnp.where(low, pltpu.roll(u, 64, 1), v).astype(BF)

    @pl.when(step == CHUNKS - 1)
    def _():
        for m in range(4):
            block = order[m]
            for q in range(4):
                y = jnp.dot(table[...], rows[4 * block + q], preferred_element_type=F32)
                cols = slice(q * 256, q * 256 + 256)
                outs[m][:, cols] = (y * inv[block, :, cols]).astype(BF)


def corr(place, order, pieces, own, rot, inv, table):
    here = pl.BlockSpec((KC, SUB, 128), lambda i, p, o: (p[i], 0, 0))
    return pl.pallas_call(
        corr_kernel,
        grid_spec=pltpu.PrefetchScalarGridSpec(
            num_scalar_prefetch=2,
            grid=(CHUNKS,),
            in_specs=[pl.BlockSpec(memory_space=pl.ANY)] * CHUNKS
            + [
                here,
                here,
                pl.BlockSpec((4, 1, 1024), lambda i, p, o: (0, 0, 0)),
                pl.BlockSpec((LAGS, 2 * BINS), lambda i, p, o: (0, 0)),
            ],
            out_specs=[pl.BlockSpec((LAGS, 1024), lambda i, p, o: (0, 0))] * 4,
            scratch_shapes=[
                pltpu.VMEM((CHUNKS, KC, SUB, 128), BF),
                pltpu.VMEM((KC, BLOCK, 128), F32),
                pltpu.VMEM((BLOCK // 4, 2 * BINS, 256), BF),
                pltpu.SemaphoreType.DMA((CHUNKS,)),
            ],
        ),
        out_shape=[jax.ShapeDtypeStruct((LAGS, 1024), BF)] * 4,
        compiler_params=VMEM,
        cost_estimate=pl.CostEstimate(flops=22 * 10**9, bytes_accessed=40 * 10**6, transcendentals=0),
        name="corr",
    )(place, order, *pieces, own, rot, inv, table)


def finish_kernel(a, b, c, *refs):
    total = a[...].astype(F32) + b[...].astype(F32) + c[...].astype(F32)
    refs[-1][0] = total.T.astype(BF)


def finish(step, near, near_got, far_sum, base=None):
    cols = 512
    extra = [] if base is None else [base]
    return pl.pallas_call(
        finish_kernel,
        grid=(1024 // cols,),
        in_specs=[pl.BlockSpec((LAGS, cols), lambda j: (0, j))] * 3
        + [pl.BlockSpec(memory_space=pl.ANY)] * len(extra),
        out_specs=pl.BlockSpec((1, cols, LAGS), lambda j: (step, j, 0)),
        out_shape=jax.ShapeDtypeStruct((STEPS, 1024, LAGS), BF),
        input_output_aliases={3: 0} if extra else {},
        compiler_params=VMEM,
        name="finish",
    )(near, near_got, far_sum, *extra)


def lag_table():
    k = np.arange(1, BINS + 1)[None, :]
    tau = np.arange(LAGS)[:, None] - LAGS // 2
    ph = ((k * tau) % NFFT) * (2 * np.pi / NFFT)
    w = np.concatenate([np.cos(ph), -np.sin(ph)], axis=1) / math.sqrt(BINS)
    return jnp.asarray(w, BF)


def along_x(a, d):
    return lax.ppermute(a, "station", [(s, s - s % 4 + (s + d) % 4) for s in range(32)])


def along_z(a, d):
    return lax.ppermute(a, "station", [(s, (s + 8 * d) % 32) for s in range(32)])


def swap_y(a):
    return lax.ppermute(a, "station", [(s, s ^ 4) for s in range(32)])


def cut(a, index, size):
    return lax.dynamic_slice_in_dim(a, index * size, size, 0)


def pick(which, options):
    out = options[0]
    for n in range(1, 4):
        out = jnp.where(which == n, options[n], out)
    return out


def barrier(*arrays):
    return lax.optimization_barrier(arrays)


def spread(sends, shifts, work=None, args=()):
    n = len(sends)
    held = barrier(*sends, *args)
    got = [shift(a) for a, shift in zip(held[:n], shifts)]
    done = list(work(*held[n:])) if work else []
    return barrier(*got, *done)


HOPS = (1, 2, 3)
TO_X = [lambda a, d=d: along_x(a, d) for d in HOPS]
TO_Z = [lambda a, d=d: along_z(a, d) for d in HOPS]


def broadcast(own, ready, marks, roots, z, h, x):
    got = spread(ready, TO_X + TO_Z)

    def own_a(q):
        return lambda ins, s: ins[0].at[pl.ds(s[4] * 64 + s[q] * 16, 16)]

    def own_b(q):
        return lambda ins, s: ins[0].at[pl.ds(s[5] * 64 + s[q] * 16, 16)]

    def came(n, q):
        return lambda ins, s: ins[n].at[pl.ds(s[q] * 16, 16)]

    scalars = jnp.stack(
        [(x - r[2]) & 3 for r in roots]
        + [(z - r[0]) & 3 for r in roots]
        + [x, 4 + z]
        + [(z + d) & 3 for d in range(4)]
        + [(x + d) & 3 for d in range(4)]
    ).astype(jnp.int32)
    tasks = []
    for d in range(4):
        for i in range(STEPS):
            tasks.append(
                (lambda outs, d=d, i=i: outs[d].at[i], i, [own_a(6 + d)] + [came(n, 6 + d) for n in (1, 2, 3)])
            )
            tasks.append(
                (lambda outs, d=d, i=i: outs[4 + d].at[i], 2 + i, [own_b(10 + d)] + [came(n, 10 + d) for n in (4, 5, 6)])
            )
    cuts = choose(scalars, [own, *got], [(STEPS, 16, SUB, 128)] * 8, tasks)
    got = spread(cuts[1:4] + cuts[5:], TO_Z + TO_X)
    got_a = [cuts[0], *got[:3]]
    got_b = [cuts[4], *got[3:]]
    mine = jnp.stack(
        [
            jnp.stack([pick((z - r[0]) & 3, [g[i] for g in got_a]) for i, r in enumerate(roots)]),
            jnp.stack([pick((x - r[2]) & 3, [g[i] for g in got_b]) for i, r in enumerate(roots)]),
        ]
    )

    def hops(marks):
        for shift in (TO_X[1], TO_Z[0]):
            marks = jnp.stack([marks, shift(marks)])
        return [marks]

    other, marks = spread([mine], [swap_y], hops, [marks])
    sub = [
        jnp.stack([jnp.where(h == r[1], mine[n, i], other[n, i]) for i, r in enumerate(roots)])
        for n in range(2)
    ]
    got = spread([sub[0]] * 3 + [sub[1]] * 3, TO_Z + TO_X)
    all_a = [sub[0], *got[:3]]
    all_b = [sub[1], *got[3:6]]
    out = []
    for i in range(STEPS):
        a = jnp.concatenate([pick((z - q) & 3, [v[i] for v in all_a]) for q in range(4)])
        b = jnp.concatenate([pick((x - q) & 3, [v[i] for v in all_b]) for q in range(4)])
        out.append((a, b))
    return out, marks


def other_core(a):
    return lax.ppermute(a, "tm", [(t, t ^ 1) for t in range(4)])


def other_chip(a):
    return lax.ppermute(a, "tm", [(t, t ^ 2) for t in range(4)])


def add(a, b):
    return (a.astype(F32) + b.astype(F32)).astype(BF)


def body(spectra, counts, block_ids):
    counts = counts[0]
    table = lag_table()
    station, tm = lax.axis_index("station"), lax.axis_index("tm")
    z, h, x = station >> 3, station >> 2 & 1, station & 3

    def places(*list_of):
        return jnp.stack(list_of).astype(jnp.int32)

    ahead = places(*[(x + d) & 3 for d in HOPS], *[4 + ((z + d) & 3) for d in HOPS])
    next_counts, own, *ready = spread(
        [counts], [TO_X[0]], lambda *a: whiten(*a), [ahead, spectra[0], counts]
    )
    marks = jnp.stack([counts, next_counts])
    roots = [(block_ids[i] >> 3, block_ids[i] >> 2 & 1, block_ids[i] & 3) for i in range(STEPS)]
    ((a0, b0), (a1, b1)), marks = broadcast(own, ready, marks, roots, z, h, x)

    place = places(
        *[(x + d) & 3 for d in (0, 3, 1, 2)], *[4 + ((z + d) & 3) for d in (0, 3, 1, 2)]
    )
    order = places((tm ^ 2) ^ 1, tm ^ 2, tm ^ 1, tm)

    def scales(marks):
        out = []
        for r in roots:
            dz, dx = (z - r[0]) & 3, (x - r[2]) & 3
            src_counts = marks[h ^ r[1], dz >> 1, dz & 1, dx >> 1, dx & 1]
            inv = 1.0 / jnp.minimum(src_counts[:, None], counts[None, :]).astype(F32)
            out.append(inv.reshape(4, 1, 1024))
        return out

    up, down = [TO_X[0], TO_Z[0]], [TO_X[2], TO_Z[2]]
    a0_up, b0_up, a0_down, b0_down, far_marks, rot = spread(
        [a0, b0, a0, b0, marks], up + down + [TO_Z[1]], lambda v: [turn(v)], [own]
    )
    marks = jnp.stack([marks, far_marks])
    a0_far, b0_far, a1_down, b1_down, far_marks = spread(
        [a0_up, b0_up, a1, b1, marks], up + down + [swap_y]
    )
    inv0, inv1 = scales(jnp.stack([marks, far_marks]))
    a1_up, b1_up, a1_far, b1_far, *lag0 = spread(
        [a1, b1, a1_down, b1_down],
        up + down,
        lambda *v: corr(place, order, v[:8], *v[8:], table),
        [a0, a0_up, a0_down, a0_far, b0, b0_up, b0_down, b0_far, own, rot, inv0],
    )
    far_got, near_got0 = spread([lag0[0], lag0[2]], [other_core] * 2)
    far_sum0, *lag1 = spread(
        [add(lag0[1], far_got)],
        [other_chip],
        lambda *v: corr(place, order, v[:8], *v[8:], table),
        [a1, a1_up, a1_down, a1_far, b1, b1_up, b1_down, b1_far, own, rot, inv1],
    )
    far_got, near_got1 = spread([lag1[0], lag1[2]], [other_core] * 2)
    far_sum1, out = spread(
        [add(lag1[1], far_got)],
        [other_chip],
        lambda *v: [finish(0, *v)],
        [lag0[3], near_got0, far_sum0],
    )
    out = finish(1, lag1[3], near_got1, far_sum1, out)
    return out.reshape(STEPS, 16, BLOCK, LAGS)


def solution(mesh):
    from jax.sharding import PartitionSpec as P

    return jax.shard_map(
        body,
        mesh=mesh,
        in_specs=(P("tm", None, "station", None), P("tm", "station"), P()),
        out_specs=P(None, "tm", "station", None),
        check_vma=False,
    )
```

```python
import math

import jax
import jax.numpy as jnp
import numpy as np
from jax import lax
from jax.experimental import pallas as pl
from jax.experimental.pallas import tpu as pltpu

NFFT, BINS, LAGS, BLOCK, STEPS, SUB = 2048, 512, 512, 64, 2, 48
EPS = 1e-6
F32, BF = jnp.float32, jnp.bfloat16
VMEM = pltpu.CompilerParams(vmem_limit_bytes=56 * 2**20)
SB = 16
KC = 64
CHUNKS = BINS // KC
HALF = BINS // 2


def whiten_kernel(place, spec, counts, *refs):
    own, pieces, work = refs[0], refs[1:-1], refs[-1]
    base = pl.program_id(0) * SB
    live = jnp.concatenate([counts[...]] * 2, axis=1)
    for s in range(SB):
        v = spec[s].astype(F32)
        power = jnp.mean(v * v, axis=-1, keepdims=True)
        n = v * lax.rsqrt(power + EPS)
        mask = (base + s < live).astype(F32)
        work[s] = jnp.concatenate([n[:, :BINS], n[:, BINS:]], axis=0).T * mask
    own[...] = jnp.swapaxes(work[...], 0, 1).astype(BF)
    for m, piece in enumerate(pieces):
        piece[:KC] = own[pl.ds(pl.multiple_of(place[m] * KC, KC), KC)]
        if m % 2 == 0:
            piece[KC] = jnp.broadcast_to(live.astype(F32), (SB, 128)).astype(BF)


def whiten(place, spectra, counts):
    n = place.shape[0]
    sizes = [KC + 1 - m % 2 for m in range(n)]
    return pl.pallas_call(
        whiten_kernel,
        grid_spec=pltpu.PrefetchScalarGridSpec(
            num_scalar_prefetch=1,
            grid=(SUB // SB,),
            in_specs=[
                pl.BlockSpec((SB, BLOCK, 2 * BINS), lambda i, p: (i, 0, 0)),
                pl.BlockSpec((1, BLOCK), lambda i, p: (0, 0)),
            ],
            out_specs=[pl.BlockSpec((BINS, SB, 128), lambda i, p: (0, i, 0))]
            + [pl.BlockSpec((size, SB, 128), lambda i, p: (0, i, 0)) for size in sizes],
            scratch_shapes=[pltpu.VMEM((SB, BINS, 128), F32)],
        ),
        out_shape=[jax.ShapeDtypeStruct((BINS, SUB, 128), BF)]
        + [jax.ShapeDtypeStruct((size, SUB, 128), BF) for size in sizes],
        compiler_params=VMEM,
        cost_estimate=pl.CostEstimate(flops=10**8, bytes_accessed=18 * 10**6, transcendentals=0),
        name="whiten",
    )(place, spectra, counts)


def choose(scalars, inputs, shapes, tasks):
    n = len(inputs)

    def kernel(*refs):
        s, ins, outs, sems = refs[0], refs[1 : 1 + n], refs[1 + n : -1], refs[-1]
        copies = []
        for m, (dst, which, sources) in enumerate(tasks):
            options = [pltpu.make_async_copy(src(ins, s), dst(outs), sems.at[m]) for src in sources]
            for number, copy in enumerate(options):
                @pl.when(s[which] == number)
                def _(copy=copy):
                    copy.start()
            copies.append(options[0])
        for copy in copies:
            copy.wait()

    anywhere = pl.BlockSpec(memory_space=pl.ANY)
    return pl.pallas_call(
        kernel,
        grid_spec=pltpu.PrefetchScalarGridSpec(
            num_scalar_prefetch=1,
            grid=(1,),
            in_specs=[anywhere] * n,
            out_specs=[pl.BlockSpec(shape, lambda i, s, n=len(shape): (0,) * n) for shape in shapes],
            scratch_shapes=[pltpu.SemaphoreType.DMA((len(tasks),))],
        ),
        out_shape=[jax.ShapeDtypeStruct(shape, BF) for shape in shapes],
        compiler_params=VMEM,
        cost_estimate=pl.CostEstimate(flops=10**6, bytes_accessed=6 * 10**6, transcendentals=0),
        name="choose",
    )(scalars, *inputs)


def turn_kernel(own, rot):
    v = own[...]
    rot[...] = jnp.concatenate([v[..., BLOCK:], -v[..., :BLOCK]], axis=-1)


def turn(own):
    blk = pl.BlockSpec((KC, SUB, 128), lambda i: (i, 0, 0))
    return pl.pallas_call(
        turn_kernel,
        grid=(CHUNKS,),
        in_specs=[blk],
        out_specs=blk,
        out_shape=jax.ShapeDtypeStruct((BINS, SUB, 128), BF),
        compiler_params=VMEM,
        cost_estimate=pl.CostEstimate(flops=10**6, bytes_accessed=25 * 10**6, transcendentals=0),
        name="turn",
    )(own)


def products(src, own, rot, work, rows):
    zero = jnp.zeros((SUB, 128), BF)

    def diagonal(a, b):
        return jnp.concatenate(
            [jnp.concatenate([a, zero], axis=1), jnp.concatenate([zero, b], axis=1)], axis=0
        )

    for e in range(2):
        for k in range(0, KC, 2):
            x = src[e, k : k + 2].reshape(2 * SUB, 128).T
            h = jnp.dot(x[:BLOCK], diagonal(own[e][k], own[e][k + 1]), preferred_element_type=F32)
            h += jnp.dot(x[BLOCK:], diagonal(rot[e][k], rot[e][k + 1]), preferred_element_type=F32)
            work[e * KC + k] = h[:, :128]
            work[e * KC + k + 1] = h[:, 128:]
    z = jnp.swapaxes(work[...], 0, 1)
    low = lax.broadcasted_iota(jnp.int32, (2 * KC, 128), 1) < BLOCK
    for p in range(BLOCK // 2):
        u, v = z[2 * p], z[2 * p + 1]
        lanes = slice(p % 2 * 128, p % 2 * 128 + 128)
        rows[p // 2, 0, :, lanes] = jnp.where(low, u, pltpu.roll(v, 64, 1)).astype(BF)
        rows[p // 2, 1, :, lanes] = jnp.where(low, pltpu.roll(u, 64, 1), v).astype(BF)


def fetch(step, pieces, src, sems):
    copies = [pltpu.make_async_copy(piece, src.at[m], sems.at[m]) for m, piece in enumerate(pieces)]

    @pl.when(step == 0)
    def _():
        for copy in copies:
            copy.start()

    for m, copy in enumerate(copies):
        @pl.when(step == m // 2)
        def _(copy=copy):
            copy.wait()


def cross_kernel(n, place, *refs):
    pieces, own, rot, rows = refs[:n], refs[n : n + 2], refs[n + 2 : n + 4], refs[n + 4]
    src, work, sems = refs[n + 5 :]
    step = pl.program_id(0)
    fetch(step, pieces, src, sems)
    products(src.at[pl.ds(2 * step, 2)], own, rot, work, rows)


def beside(n):
    return [
        pl.BlockSpec((KC, SUB, 128), lambda i, p, *_, e=e: (p[jnp.minimum(2 * i, n - 2) + e], 0, 0))
        for e in range(2)
    ]


def cross(place, pieces, own, rot):
    n = len(pieces)
    return pl.pallas_call(
        lambda *refs: cross_kernel(n, *refs),
        grid_spec=pltpu.PrefetchScalarGridSpec(
            num_scalar_prefetch=1,
            grid=(n // 2,),
            in_specs=[pl.BlockSpec(memory_space=pl.ANY)] * n + beside(n) * 2,
            out_specs=pl.BlockSpec((BLOCK // 4, 2, 2 * KC, 256), lambda i, p: (0, 0, i, 0)),
            scratch_shapes=[
                pltpu.VMEM((n, KC, SUB, 128), BF),
                pltpu.VMEM((2 * KC, BLOCK, 128), F32),
                pltpu.SemaphoreType.DMA((n,)),
            ],
        ),
        out_shape=jax.ShapeDtypeStruct((BLOCK // 4, 2, n * KC, 256), BF),
        compiler_params=VMEM,
        cost_estimate=pl.CostEstimate(flops=n * 10**9, bytes_accessed=n * 4 * 10**6, transcendentals=0),
        name="cross",
    )(place, *pieces, own, own, rot, rot)


def corr_kernel(n, done, place, order, *refs):
    pieces, own, rot = refs[:n], refs[n : n + 2], refs[n + 2 : n + 4]
    inv, table = refs[n + 4 : n + 6]
    first = refs[n + 6] if done else None
    refs = refs[n + 6 + bool(done) :]
    outs, (src, work, rows, lag, sems, out_sems) = refs[:4], refs[4:]
    step = pl.program_id(0)
    steps = n // 2
    fetch(step, pieces, src, sems)
    for i in range(steps):
        @pl.when(step == i)
        def _(i=i):
            products(src.at[2 * i : 2 * i + 2], own, rot, work, rows.at[:, :, i * 2 * KC : (i + 1) * 2 * KC])

    for m in range(4):
        @pl.when(step == steps + m)
        def _(m=m):
            block = order[m]
            for q in range(4):
                parts = []
                for c in range(2):
                    if done:
                        parts.append(first[q, c])
                    parts.append(rows[4 * block + q, c])
                y = jnp.dot(table[...], jnp.concatenate(parts, axis=0), preferred_element_type=F32)
                cols = slice(q * 256, q * 256 + 256)
                lag[m, :, cols] = (y * inv[block, :, cols]).astype(BF)
            pltpu.make_async_copy(lag.at[m], outs[m], out_sems.at[m]).start()

    @pl.when(step == steps + 3)
    def _():
        for m in range(4):
            pltpu.make_async_copy(lag.at[m], outs[m], out_sems.at[m]).wait()


def corr(place, order, pieces, own, rot, inv, table, first=None):
    n = len(pieces)
    done = 0 if first is None else first.shape[2]
    anywhere = pl.BlockSpec(memory_space=pl.ANY)
    extra, extra_specs = [], []
    if done:
        extra = [first]
        extra_specs = [
            pl.BlockSpec((4, 2, done, 256), lambda i, p, o: (o[jnp.clip(i - n // 2, 0, 3)], 0, 0, 0))
        ]
    return pl.pallas_call(
        lambda *refs: corr_kernel(n, done, *refs),
        grid_spec=pltpu.PrefetchScalarGridSpec(
            num_scalar_prefetch=2,
            grid=(n // 2 + 4,),
            in_specs=[anywhere] * n
            + beside(n) * 2
            + [
                pl.BlockSpec((4, 1, 1024), lambda i, p, o: (0, 0, 0)),
                pl.BlockSpec((LAGS, 2 * BINS), lambda i, p, o: (0, 0)),
            ]
            + extra_specs,
            out_specs=[anywhere] * 4,
            scratch_shapes=[
                pltpu.VMEM((n, KC, SUB, 128), BF),
                pltpu.VMEM((2 * KC, BLOCK, 128), F32),
                pltpu.VMEM((BLOCK // 4, 2, n * KC, 256), BF),
                pltpu.VMEM((4, LAGS, 1024), BF),
                pltpu.SemaphoreType.DMA((n,)),
                pltpu.SemaphoreType.DMA((4,)),
            ],
        ),
        out_shape=[jax.ShapeDtypeStruct((LAGS, 1024), BF)] * 4,
        compiler_params=VMEM,
        cost_estimate=pl.CostEstimate(flops=(n + 6) * 10**9, bytes_accessed=n * 5 * 10**6, transcendentals=0),
        name="corr",
    )(place, order, *pieces, own, own, rot, rot, inv, table, *extra)


def finish_kernel(a, b, c, *refs):
    total = a[...].astype(F32) + b[...].astype(F32) + c[...].astype(F32)
    refs[-1][0] = total.T.astype(BF)


def finish(step, near, near_got, far_sum, base=None):
    cols = 512
    extra = [] if base is None else [base]
    return pl.pallas_call(
        finish_kernel,
        grid=(1024 // cols,),
        in_specs=[pl.BlockSpec((LAGS, cols), lambda j: (0, j))] * 3
        + [pl.BlockSpec(memory_space=pl.ANY)] * len(extra),
        out_specs=pl.BlockSpec((1, cols, LAGS), lambda j: (step, j, 0)),
        out_shape=jax.ShapeDtypeStruct((STEPS, 1024, LAGS), BF),
        input_output_aliases={3: 0} if extra else {},
        compiler_params=pltpu.CompilerParams(vmem_limit_bytes=63 * 2**20),
        name="finish",
    )(near, near_got, far_sum, *extra)


def arrange_kernel(place, left, right, out):
    out[...] = jnp.concatenate([left[0, 0], right[0, 0]], axis=1)


def arrange(place, table):
    return pl.pallas_call(
        arrange_kernel,
        grid_spec=pltpu.PrefetchScalarGridSpec(
            num_scalar_prefetch=1,
            grid=(CHUNKS,),
            in_specs=[
                pl.BlockSpec((1, 1, LAGS, KC), lambda i, p, e=e: (i // 4, p[i % 4 * 2 + e], 0, 0))
                for e in range(2)
            ],
            out_specs=pl.BlockSpec((LAGS, 2 * KC), lambda i, p: (0, i)),
        ),
        out_shape=jax.ShapeDtypeStruct((LAGS, 2 * BINS), BF),
        compiler_params=VMEM,
        cost_estimate=pl.CostEstimate(flops=10**6, bytes_accessed=25 * 10**6, transcendentals=0),
        name="arrange",
    )(place, table, table)


def lag_table():
    k = np.arange(1, BINS + 1)[None, :]
    tau = np.arange(LAGS)[:, None] - LAGS // 2
    ph = ((k * tau) % NFFT) * (2 * np.pi / NFFT)
    w = np.stack([np.cos(ph), -np.sin(ph)]) / math.sqrt(BINS)
    return jnp.asarray(w.reshape(2, LAGS, CHUNKS, KC).transpose(0, 2, 1, 3), BF)


def along_x(a, d):
    return lax.ppermute(a, "station", [(s, s - s % 4 + (s + d) % 4) for s in range(32)])


def along_z(a, d):
    return lax.ppermute(a, "station", [(s, (s + 8 * d) % 32) for s in range(32)])


def swap_y(a):
    return lax.ppermute(a, "station", [(s, s ^ 4) for s in range(32)])


def cut(a, index, size):
    return lax.dynamic_slice_in_dim(a, index * size, size, 0)


def pick(which, options):
    out = options[0]
    for n in range(1, 4):
        out = jnp.where(which == n, options[n], out)
    return out


def barrier(*arrays):
    return lax.optimization_barrier(arrays)


def spread(sends, shifts, work=None, args=()):
    n = len(sends)
    held = barrier(*sends, *args)
    got = [shift(a) for a, shift in zip(held[:n], shifts)]
    done = list(work(*held[n:])) if work else []
    return barrier(*got, *done)


HOPS = (2, 1, 3)
TO_X = {d: lambda a, d=d: along_x(a, d) for d in HOPS}
TO_Z = {d: lambda a, d=d: along_z(a, d) for d in HOPS}
X_THEN_Z = [to[d] for d in HOPS for to in (TO_X, TO_Z)]
Z_THEN_X = [to[d] for d in HOPS for to in (TO_Z, TO_X)]


def by_hop(got):
    return [[got[2 * HOPS.index(d) + n] for d in (1, 2, 3)] for n in range(2)]


def broadcast(own, ready, counts, roots, z, h, x, beside):
    from_x, from_z = by_hop(spread(ready, X_THEN_Z))

    def own_a(q):
        return lambda ins, s: ins[0].at[pl.ds(s[4] * 64 + s[q] * 16, 16)]

    def own_b(q):
        return lambda ins, s: ins[0].at[pl.ds(s[5] * 64 + s[q] * 16, 16)]

    def came(n, q):
        return lambda ins, s: ins[n].at[pl.ds(s[q] * 16, 16)]

    def row(n):
        return lambda ins, s: ins[n].at[64:65]

    scalars = jnp.stack(
        [(x - r[2]) & 3 for r in roots]
        + [(z - r[0]) & 3 for r in roots]
        + [x, 4 + z]
        + [(z + d) & 3 for d in range(4)]
        + [(x + d) & 3 for d in range(4)]
    ).astype(jnp.int32)
    tasks = []
    for d in range(4):
        for i in range(STEPS):
            tasks += [
                (lambda outs, d=d, i=i: outs[d].at[i, :16], i, [own_a(6 + d)] + [came(n, 6 + d) for n in (2, 3, 4)]),
                (lambda outs, d=d, i=i: outs[d].at[i, 16:], i, [row(n) for n in (1, 2, 3, 4)]),
                (lambda outs, d=d, i=i: outs[4 + d].at[i], 2 + i, [own_b(10 + d)] + [came(n, 10 + d) for n in (5, 6, 7)]),
            ]
    shapes = [(STEPS, 17, SUB, 128)] * 4 + [(STEPS, 16, SUB, 128)] * 4
    cuts = choose(scalars, [own, ready[0], *from_x, *from_z], shapes, tasks)
    got = spread(
        cuts[1:4] + cuts[5:], [TO_Z[d] for d in (1, 2, 3)] + [TO_X[d] for d in (1, 2, 3)]
    )
    got_a = [cuts[0], *got[:3]]
    got_b = [cuts[4], *got[3:]]
    mine = jnp.stack(
        [
            jnp.concatenate(
                [pick((z - r[0]) & 3, [g[i] for g in got_a]), pick((x - r[2]) & 3, [g[i] for g in got_b])]
            )
            for i, r in enumerate(roots)
        ]
    )
    other, table = spread([mine], [swap_y], *beside)
    here = [h == r[1] for r in roots]
    sub = [
        jnp.stack([jnp.where(here[i], mine[i, rows], other[i, rows]) for i in range(STEPS)])
        for rows in (slice(0, 16), slice(17, 33))
    ]

    def scales(mine, other):
        out = []
        for i in range(STEPS):
            src_counts = jnp.where(here[i], mine[i, 16, 0, :BLOCK], other[i, 16, 0, :BLOCK]).astype(F32)
            inv = 1.0 / jnp.minimum(src_counts[:, None], counts[None, :].astype(F32))
            out.append(inv.reshape(4, 1, 1024))
        return out

    from_z, from_x = by_hop(spread(sub * 3, Z_THEN_X))
    all_a = [sub[0], *from_z]
    all_b = [sub[1], *from_x]
    out = []
    for i in range(STEPS):
        a = jnp.concatenate([pick((z - q) & 3, [v[i] for v in all_a]) for q in range(4)])
        b = jnp.concatenate([pick((x - q) & 3, [v[i] for v in all_b]) for q in range(4)])
        out.append((a, b))
    return out, table, scales, [mine, other]


def other_core(a):
    return lax.ppermute(a, "tm", [(t, t ^ 1) for t in range(4)])


def other_chip(a):
    return lax.ppermute(a, "tm", [(t, t ^ 2) for t in range(4)])


def add(a, b):
    return (a.astype(F32) + b.astype(F32)).astype(BF)


def body(spectra, counts, block_ids):
    station, tm = lax.axis_index("station"), lax.axis_index("tm")
    z, h, x = station >> 3, station >> 2 & 1, station & 3

    def places(*list_of):
        return jnp.stack(list_of).astype(jnp.int32)

    ahead = places(*[v for d in HOPS for v in ((x + d) & 3, 4 + ((z + d) & 3))])
    own, *ready = whiten(ahead, spectra[0], counts)
    roots = [(block_ids[i] >> 3, block_ids[i] >> 2 & 1, block_ids[i] & 3) for i in range(STEPS)]
    place = places(
        x, (x + 3) & 3, 4 + z, 4 + ((z + 3) & 3), (x + 1) & 3, (x + 2) & 3, 4 + ((z + 1) & 3), 4 + ((z + 2) & 3)
    )

    ((a0, b0), (a1, b1)), table, scales, scales_of = broadcast(
        own, ready, counts[0], roots, z, h, x, (lambda *a: [arrange(*a)], [place, lag_table()])
    )
    order = places((tm ^ 2) ^ 1, tm ^ 2, tm ^ 1, tm)

    up, down = [TO_X[1], TO_Z[1]], [TO_X[3], TO_Z[3]]
    a0_up, b0_up, a0_down, b0_down, rot = spread(
        [a0, b0, a0, b0], up + down, lambda v: [turn(v)], [own]
    )
    def work(mine, other, *v):
        return [*scales(mine, other), cross(place[:4], v[:4], *v[4:])]

    a0_far, b0_far, a1_down, b1_down, inv0, inv1, first = spread(
        [a0_up, b0_up, a1, b1], up + down, work, [*scales_of, a0, a0_up, b0, b0_up, own, rot]
    )
    a1_up, b1_up, a1_far, b1_far, *lag0 = spread(
        [a1, b1, a1_down, b1_down],
        up + down,
        lambda first, *v: corr(place[4:], order, v[:4], *v[4:], table, first),
        [first, a0_down, a0_far, b0_down, b0_far, own, rot, inv0],
    )
    (far_got,) = spread([lag0[0]], [other_core])
    far_sum0, near_got0, *lag1 = spread(
        [add(lag0[1], far_got), lag0[2]],
        [other_chip, other_core],
        lambda *v: corr(place, order, v[:8], *v[8:], table),
        [a1, a1_up, b1, b1_up, a1_down, a1_far, b1_down, b1_far, own, rot, inv1],
    )
    (far_got,) = spread([lag1[0]], [other_core])
    far_sum1, near_got1, out = spread(
        [add(lag1[1], far_got), lag1[2]],
        [other_chip, other_core],
        lambda *v: [finish(0, *v)],
        [lag0[3], near_got0, far_sum0],
    )
    out = finish(1, lag1[3], near_got1, far_sum1, out)
    return out.reshape(STEPS, 16, BLOCK, LAGS)


def solution(mesh):
    from jax.sharding import PartitionSpec as P

    return jax.shard_map(
        body,
        mesh=mesh,
        in_specs=(P("tm", None, "station", None), P("tm", "station"), P()),
        out_specs=P(None, "tm", "station", None),
        check_vma=False,
    )
```

```python
import math

import jax
import jax.numpy as jnp
import numpy as np
from jax import lax
from jax.experimental import pallas as pl
from jax.experimental.pallas import tpu as pltpu

NFFT, BINS, LAGS, BLOCK, STEPS, SUB = 2048, 512, 512, 64, 2, 48
EPS = 1e-6
F32, BF = jnp.float32, jnp.bfloat16
VMEM = pltpu.CompilerParams(vmem_limit_bytes=56 * 2**20)
SB = 16
KC = 64
CHUNKS = BINS // KC
HALF = BINS // 2


def whiten_kernel(place, spec, counts, *refs):
    own, pieces, work = refs[0], refs[1:-1], refs[-1]
    base = pl.program_id(0) * SB
    live = jnp.concatenate([counts[...]] * 2, axis=1)
    for s in range(SB):
        v = spec[s].astype(F32)
        power = jnp.mean(v * v, axis=-1, keepdims=True)
        n = v * lax.rsqrt(power + EPS)
        mask = (base + s < live).astype(F32)
        work[s] = jnp.concatenate([n[:, :BINS], n[:, BINS:]], axis=0).T * mask
    own[...] = jnp.swapaxes(work[...], 0, 1).astype(BF)
    for m, piece in enumerate(pieces):
        piece[:KC] = own[pl.ds(pl.multiple_of(place[m] * KC, KC), KC)]
        if m % 2 == 0:
            piece[KC] = jnp.broadcast_to(live.astype(F32), (SB, 128)).astype(BF)


def whiten(place, spectra, counts):
    n = place.shape[0]
    sizes = [KC + 1 - m % 2 for m in range(n)]
    return pl.pallas_call(
        whiten_kernel,
        grid_spec=pltpu.PrefetchScalarGridSpec(
            num_scalar_prefetch=1,
            grid=(SUB // SB,),
            in_specs=[
                pl.BlockSpec((SB, BLOCK, 2 * BINS), lambda i, p: (i, 0, 0)),
                pl.BlockSpec((1, BLOCK), lambda i, p: (0, 0)),
            ],
            out_specs=[pl.BlockSpec((BINS, SB, 128), lambda i, p: (0, i, 0))]
            + [pl.BlockSpec((size, SB, 128), lambda i, p: (0, i, 0)) for size in sizes],
            scratch_shapes=[pltpu.VMEM((SB, BINS, 128), F32)],
        ),
        out_shape=[jax.ShapeDtypeStruct((BINS, SUB, 128), BF)]
        + [jax.ShapeDtypeStruct((size, SUB, 128), BF) for size in sizes],
        compiler_params=VMEM,
        cost_estimate=pl.CostEstimate(flops=10**8, bytes_accessed=18 * 10**6, transcendentals=0),
        name="whiten",
    )(place, spectra, counts)


def choose(scalars, inputs, shapes, tasks):
    n = len(inputs)

    def kernel(*refs):
        s, ins, outs, sems = refs[0], refs[1 : 1 + n], refs[1 + n : -1], refs[-1]
        copies = []
        for m, (dst, which, sources) in enumerate(tasks):
            options = [pltpu.make_async_copy(src(ins, s), dst(outs), sems.at[m]) for src in sources]
            for number, copy in enumerate(options):
                @pl.when(s[which] == number)
                def _(copy=copy):
                    copy.start()
            copies.append(options[0])
        for copy in copies:
            copy.wait()

    anywhere = pl.BlockSpec(memory_space=pl.ANY)
    return pl.pallas_call(
        kernel,
        grid_spec=pltpu.PrefetchScalarGridSpec(
            num_scalar_prefetch=1,
            grid=(1,),
            in_specs=[anywhere] * n,
            out_specs=[pl.BlockSpec(shape, lambda i, s, n=len(shape): (0,) * n) for shape in shapes],
            scratch_shapes=[pltpu.SemaphoreType.DMA((len(tasks),))],
        ),
        out_shape=[jax.ShapeDtypeStruct(shape, BF) for shape in shapes],
        compiler_params=VMEM,
        cost_estimate=pl.CostEstimate(flops=10**6, bytes_accessed=6 * 10**6, transcendentals=0),
        name="choose",
    )(scalars, *inputs)


def turn_kernel(own, rot):
    v = own[...]
    rot[...] = jnp.concatenate([v[..., BLOCK:], -v[..., :BLOCK]], axis=-1)


def turn(own):
    blk = pl.BlockSpec((KC, SUB, 128), lambda i: (i, 0, 0))
    return pl.pallas_call(
        turn_kernel,
        grid=(CHUNKS,),
        in_specs=[blk],
        out_specs=blk,
        out_shape=jax.ShapeDtypeStruct((BINS, SUB, 128), BF),
        compiler_params=VMEM,
        cost_estimate=pl.CostEstimate(flops=10**6, bytes_accessed=25 * 10**6, transcendentals=0),
        name="turn",
    )(own)


def corr_kernel(place, order, *refs):
    pieces = refs[:CHUNKS]
    own, rot = refs[CHUNKS : CHUNKS + 2], refs[CHUNKS + 2 : CHUNKS + 4]
    inv, table = refs[CHUNKS + 4 : CHUNKS + 6]
    outs = refs[CHUNKS + 6 : CHUNKS + 10]
    src, work, rows, sems = refs[CHUNKS + 10 :]
    step = pl.program_id(0)
    copies = [pltpu.make_async_copy(piece, src.at[m], sems.at[m]) for m, piece in enumerate(pieces)]

    @pl.when(step == 0)
    def _():
        for copy in copies:
            copy.start()

    for m, copy in enumerate(copies):
        @pl.when(step == m // 2)
        def _(copy=copy):
            copy.wait()

    zero = jnp.zeros((SUB, 128), BF)

    def diagonal(a, b):
        return jnp.concatenate(
            [jnp.concatenate([a, zero], axis=1), jnp.concatenate([zero, b], axis=1)], axis=0
        )

    for e in range(2):
        for k in range(0, KC, 2):
            x = src[2 * step + e, k : k + 2].reshape(2 * SUB, 128).T
            h = jnp.dot(x[:BLOCK], diagonal(own[e][k], own[e][k + 1]), preferred_element_type=F32)
            h += jnp.dot(x[BLOCK:], diagonal(rot[e][k], rot[e][k + 1]), preferred_element_type=F32)
            work[e * KC + k] = h[:, :128]
            work[e * KC + k + 1] = h[:, 128:]
    z = jnp.swapaxes(work[...], 0, 1)
    low = lax.broadcasted_iota(jnp.int32, (2 * KC, 128), 1) < BLOCK
    offs = [pl.multiple_of(place[2 * step + e] * KC, KC) for e in range(2)]
    for p in range(BLOCK // 2):
        u, v = z[2 * p], z[2 * p + 1]
        lanes = slice(p % 2 * 128, p % 2 * 128 + 128)
        re = jnp.where(low, u, pltpu.roll(v, 64, 1)).astype(BF)
        im = jnp.where(low, pltpu.roll(u, 64, 1), v).astype(BF)
        for e in range(2):
            rows[p // 2, pl.ds(offs[e], KC), lanes] = re[e * KC : e * KC + KC]
            rows[p // 2, pl.ds(offs[e] + BINS, KC), lanes] = im[e * KC : e * KC + KC]

    @pl.when(step == CHUNKS // 2 - 1)
    def _():
        for m in range(4):
            block = order[m]
            for q in range(4):
                y = jnp.dot(table[...], rows[4 * block + q], preferred_element_type=F32)
                cols = slice(q * 256, q * 256 + 256)
                outs[m][:, cols] = (y * inv[block, :, cols]).astype(BF)


def corr(place, order, pieces, own, rot, inv, table):
    here = [pl.BlockSpec((KC, SUB, 128), lambda i, p, o, e=e: (p[2 * i + e], 0, 0)) for e in range(2)]
    return pl.pallas_call(
        corr_kernel,
        grid_spec=pltpu.PrefetchScalarGridSpec(
            num_scalar_prefetch=2,
            grid=(CHUNKS // 2,),
            in_specs=[pl.BlockSpec(memory_space=pl.ANY)] * CHUNKS
            + here * 2
            + [
                pl.BlockSpec((4, 1, 1024), lambda i, p, o: (0, 0, 0)),
                pl.BlockSpec((LAGS, 2 * BINS), lambda i, p, o: (0, 0)),
            ],
            out_specs=[pl.BlockSpec((LAGS, 1024), lambda i, p, o: (0, 0))] * 4,
            scratch_shapes=[
                pltpu.VMEM((CHUNKS, KC, SUB, 128), BF),
                pltpu.VMEM((2 * KC, BLOCK, 128), F32),
                pltpu.VMEM((BLOCK // 4, 2 * BINS, 256), BF),
                pltpu.SemaphoreType.DMA((CHUNKS,)),
            ],
        ),
        out_shape=[jax.ShapeDtypeStruct((LAGS, 1024), BF)] * 4,
        compiler_params=VMEM,
        cost_estimate=pl.CostEstimate(flops=22 * 10**9, bytes_accessed=40 * 10**6, transcendentals=0),
        name="corr",
    )(place, order, *pieces, own, own, rot, rot, inv, table)


def finish_kernel(a, b, c, *refs):
    total = a[...].astype(F32) + b[...].astype(F32) + c[...].astype(F32)
    refs[-1][0] = total.T.astype(BF)


def finish(step, near, near_got, far_sum, base=None):
    cols = 512
    extra = [] if base is None else [base]
    return pl.pallas_call(
        finish_kernel,
        grid=(1024 // cols,),
        in_specs=[pl.BlockSpec((LAGS, cols), lambda j: (0, j))] * 3
        + [pl.BlockSpec(memory_space=pl.ANY)] * len(extra),
        out_specs=pl.BlockSpec((1, cols, LAGS), lambda j: (step, j, 0)),
        out_shape=jax.ShapeDtypeStruct((STEPS, 1024, LAGS), BF),
        input_output_aliases={3: 0} if extra else {},
        compiler_params=VMEM,
        name="finish",
    )(near, near_got, far_sum, *extra)


def lag_table():
    k = np.arange(1, BINS + 1)[None, :]
    tau = np.arange(LAGS)[:, None] - LAGS // 2
    ph = ((k * tau) % NFFT) * (2 * np.pi / NFFT)
    w = np.concatenate([np.cos(ph), -np.sin(ph)], axis=1) / math.sqrt(BINS)
    return jnp.asarray(w, BF)


def along_x(a, d):
    return lax.ppermute(a, "station", [(s, s - s % 4 + (s + d) % 4) for s in range(32)])


def along_z(a, d):
    return lax.ppermute(a, "station", [(s, (s + 8 * d) % 32) for s in range(32)])


def swap_y(a):
    return lax.ppermute(a, "station", [(s, s ^ 4) for s in range(32)])


def cut(a, index, size):
    return lax.dynamic_slice_in_dim(a, index * size, size, 0)


def pick(which, options):
    out = options[0]
    for n in range(1, 4):
        out = jnp.where(which == n, options[n], out)
    return out


def barrier(*arrays):
    return lax.optimization_barrier(arrays)


def spread(sends, shifts, work=None, args=()):
    n = len(sends)
    held = barrier(*sends, *args)
    got = [shift(a) for a, shift in zip(held[:n], shifts)]
    done = list(work(*held[n:])) if work else []
    return barrier(*got, *done)


HOPS = (2, 1, 3)
TO_X = {d: lambda a, d=d: along_x(a, d) for d in HOPS}
TO_Z = {d: lambda a, d=d: along_z(a, d) for d in HOPS}
X_THEN_Z = [to[d] for d in HOPS for to in (TO_X, TO_Z)]
Z_THEN_X = [to[d] for d in HOPS for to in (TO_Z, TO_X)]


def by_hop(got):
    return [[got[2 * HOPS.index(d) + n] for d in (1, 2, 3)] for n in range(2)]


def broadcast(own, ready, counts, roots, z, h, x):
    from_x, from_z = by_hop(spread(ready, X_THEN_Z))

    def own_a(q):
        return lambda ins, s: ins[0].at[pl.ds(s[4] * 64 + s[q] * 16, 16)]

    def own_b(q):
        return lambda ins, s: ins[0].at[pl.ds(s[5] * 64 + s[q] * 16, 16)]

    def came(n, q):
        return lambda ins, s: ins[n].at[pl.ds(s[q] * 16, 16)]

    def row(n):
        return lambda ins, s: ins[n].at[64:65]

    scalars = jnp.stack(
        [(x - r[2]) & 3 for r in roots]
        + [(z - r[0]) & 3 for r in roots]
        + [x, 4 + z]
        + [(z + d) & 3 for d in range(4)]
        + [(x + d) & 3 for d in range(4)]
    ).astype(jnp.int32)
    tasks = []
    for d in range(4):
        for i in range(STEPS):
            tasks += [
                (lambda outs, d=d, i=i: outs[d].at[i, :16], i, [own_a(6 + d)] + [came(n, 6 + d) for n in (2, 3, 4)]),
                (lambda outs, d=d, i=i: outs[d].at[i, 16:], i, [row(n) for n in (1, 2, 3, 4)]),
                (lambda outs, d=d, i=i: outs[4 + d].at[i], 2 + i, [own_b(10 + d)] + [came(n, 10 + d) for n in (5, 6, 7)]),
            ]
    shapes = [(STEPS, 17, SUB, 128)] * 4 + [(STEPS, 16, SUB, 128)] * 4
    cuts = choose(scalars, [own, ready[0], *from_x, *from_z], shapes, tasks)
    got = spread(
        cuts[1:4] + cuts[5:], [TO_Z[d] for d in (1, 2, 3)] + [TO_X[d] for d in (1, 2, 3)]
    )
    got_a = [cuts[0], *got[:3]]
    got_b = [cuts[4], *got[3:]]
    mine = jnp.stack(
        [
            jnp.concatenate(
                [pick((z - r[0]) & 3, [g[i] for g in got_a]), pick((x - r[2]) & 3, [g[i] for g in got_b])]
            )
            for i, r in enumerate(roots)
        ]
    )
    (other,) = spread([mine], [swap_y])
    here = [h == r[1] for r in roots]
    sub = [
        jnp.stack([jnp.where(here[i], mine[i, rows], other[i, rows]) for i in range(STEPS)])
        for rows in (slice(0, 16), slice(17, 33))
    ]

    def scales(mine, other):
        out = []
        for i in range(STEPS):
            src_counts = jnp.where(here[i], mine[i, 16, 0, :BLOCK], other[i, 16, 0, :BLOCK]).astype(F32)
            inv = 1.0 / jnp.minimum(src_counts[:, None], counts[None, :].astype(F32))
            out.append(inv.reshape(4, 1, 1024))
        return out

    got = spread(sub * 3, Z_THEN_X, scales, [mine, other])
    from_z, from_x = by_hop(got[:6])
    all_a = [sub[0], *from_z]
    all_b = [sub[1], *from_x]
    out = []
    for i in range(STEPS):
        a = jnp.concatenate([pick((z - q) & 3, [v[i] for v in all_a]) for q in range(4)])
        b = jnp.concatenate([pick((x - q) & 3, [v[i] for v in all_b]) for q in range(4)])
        out.append((a, b))
    return out, got[6:]


def other_core(a):
    return lax.ppermute(a, "tm", [(t, t ^ 1) for t in range(4)])


def other_chip(a):
    return lax.ppermute(a, "tm", [(t, t ^ 2) for t in range(4)])


def add(a, b):
    return (a.astype(F32) + b.astype(F32)).astype(BF)


def body(spectra, counts, block_ids):
    station, tm = lax.axis_index("station"), lax.axis_index("tm")
    z, h, x = station >> 3, station >> 2 & 1, station & 3

    def places(*list_of):
        return jnp.stack(list_of).astype(jnp.int32)

    ahead = places(*[v for d in HOPS for v in ((x + d) & 3, 4 + ((z + d) & 3))])
    own, *ready = whiten(ahead, spectra[0], counts)
    roots = [(block_ids[i] >> 3, block_ids[i] >> 2 & 1, block_ids[i] & 3) for i in range(STEPS)]
    ((a0, b0), (a1, b1)), (inv0, inv1) = broadcast(own, ready, counts[0], roots, z, h, x)

    place = places(
        *[(x + d) & 3 for d in (0, 3, 1, 2)], *[4 + ((z + d) & 3) for d in (0, 3, 1, 2)]
    )
    table = lag_table()
    order = places((tm ^ 2) ^ 1, tm ^ 2, tm ^ 1, tm)

    up, down = [TO_X[1], TO_Z[1]], [TO_X[3], TO_Z[3]]
    a0_up, b0_up, a0_down, b0_down, rot = spread(
        [a0, b0, a0, b0], up + down, lambda v: [turn(v)], [own]
    )
    a0_far, b0_far, a1_down, b1_down = spread([a0_up, b0_up, a1, b1], up + down)
    a1_up, b1_up, a1_far, b1_far, *lag0 = spread(
        [a1, b1, a1_down, b1_down],
        up + down,
        lambda *v: corr(place, order, v[:8], *v[8:], table),
        [a0, a0_up, a0_down, a0_far, b0, b0_up, b0_down, b0_far, own, rot, inv0],
    )
    (far_got,) = spread([lag0[0]], [other_core])
    far_sum0, near_got0, *lag1 = spread(
        [add(lag0[1], far_got), lag0[2]],
        [other_chip, other_core],
        lambda *v: corr(place, order, v[:8], *v[8:], table),
        [a1, a1_up, a1_down, a1_far, b1, b1_up, b1_down, b1_far, own, rot, inv1],
    )
    (far_got,) = spread([lag1[0]], [other_core])
    far_sum1, near_got1, out = spread(
        [add(lag1[1], far_got), lag1[2]],
        [other_chip, other_core],
        lambda *v: [finish(0, *v)],
        [lag0[3], near_got0, far_sum0],
    )
    out = finish(1, lag1[3], near_got1, far_sum1, out)
    return out.reshape(STEPS, 16, BLOCK, LAGS)


def solution(mesh):
    from jax.sharding import PartitionSpec as P

    return jax.shard_map(
        body,
        mesh=mesh,
        in_specs=(P("tm", None, "station", None), P("tm", "station"), P()),
        out_specs=P(None, "tm", "station", None),
        check_vma=False,
    )
```

```python
import math

import jax
import jax.numpy as jnp
import numpy as np
from jax import lax
from jax.experimental import pallas as pl
from jax.experimental.pallas import tpu as pltpu

NFFT, BINS, LAGS, BLOCK, STEPS, SUB = 2048, 512, 512, 64, 2, 48
EPS = 1e-6
F32, BF = jnp.float32, jnp.bfloat16
VMEM = pltpu.CompilerParams(vmem_limit_bytes=56 * 2**20)
SB = 16
KC = 64
CHUNKS = BINS // KC
HALF = BINS // 2


def whiten_kernel(place, spec, counts, *refs):
    own, pieces, work = refs[0], refs[1:-1], refs[-1]
    base = pl.program_id(0) * SB
    live = jnp.concatenate([counts[...]] * 2, axis=1)
    for s in range(SB):
        v = spec[s].astype(F32)
        power = jnp.mean(v * v, axis=-1, keepdims=True)
        n = v * lax.rsqrt(power + EPS)
        mask = (base + s < live).astype(F32)
        work[s] = jnp.concatenate([n[:, :BINS], n[:, BINS:]], axis=0).T * mask
    own[...] = jnp.swapaxes(work[...], 0, 1).astype(BF)
    for m, piece in enumerate(pieces):
        piece[:KC] = own[pl.ds(pl.multiple_of(place[m] * KC, KC), KC)]
        if m % 2 == 0:
            piece[KC] = jnp.broadcast_to(live.astype(F32), (SB, 128)).astype(BF)


def whiten(place, spectra, counts):
    n = place.shape[0]
    sizes = [KC + 1 - m % 2 for m in range(n)]
    return pl.pallas_call(
        whiten_kernel,
        grid_spec=pltpu.PrefetchScalarGridSpec(
            num_scalar_prefetch=1,
            grid=(SUB // SB,),
            in_specs=[
                pl.BlockSpec((SB, BLOCK, 2 * BINS), lambda i, p: (i, 0, 0)),
                pl.BlockSpec((1, BLOCK), lambda i, p: (0, 0)),
            ],
            out_specs=[pl.BlockSpec((BINS, SB, 128), lambda i, p: (0, i, 0))]
            + [pl.BlockSpec((size, SB, 128), lambda i, p: (0, i, 0)) for size in sizes],
            scratch_shapes=[pltpu.VMEM((SB, BINS, 128), F32)],
        ),
        out_shape=[jax.ShapeDtypeStruct((BINS, SUB, 128), BF)]
        + [jax.ShapeDtypeStruct((size, SUB, 128), BF) for size in sizes],
        compiler_params=VMEM,
        cost_estimate=pl.CostEstimate(flops=10**8, bytes_accessed=18 * 10**6, transcendentals=0),
        name="whiten",
    )(place, spectra, counts)


def choose(scalars, inputs, shapes, tasks):
    n = len(inputs)

    def kernel(*refs):
        s, ins, outs, sems = refs[0], refs[1 : 1 + n], refs[1 + n : -1], refs[-1]
        copies = []
        for m, (dst, which, sources) in enumerate(tasks):
            options = [pltpu.make_async_copy(src(ins, s), dst(outs), sems.at[m]) for src in sources]
            for number, copy in enumerate(options):
                @pl.when(s[which] == number)
                def _(copy=copy):
                    copy.start()
            copies.append(options[0])
        for copy in copies:
            copy.wait()

    anywhere = pl.BlockSpec(memory_space=pl.ANY)
    return pl.pallas_call(
        kernel,
        grid_spec=pltpu.PrefetchScalarGridSpec(
            num_scalar_prefetch=1,
            grid=(1,),
            in_specs=[anywhere] * n,
            out_specs=[pl.BlockSpec(shape, lambda i, s, n=len(shape): (0,) * n) for shape in shapes],
            scratch_shapes=[pltpu.SemaphoreType.DMA((len(tasks),))],
        ),
        out_shape=[jax.ShapeDtypeStruct(shape, BF) for shape in shapes],
        compiler_params=VMEM,
        cost_estimate=pl.CostEstimate(flops=10**6, bytes_accessed=6 * 10**6, transcendentals=0),
        name="choose",
    )(scalars, *inputs)


def turn_kernel(own, rot):
    v = own[...]
    rot[...] = jnp.concatenate([v[..., BLOCK:], -v[..., :BLOCK]], axis=-1)


def turn(own):
    blk = pl.BlockSpec((KC, SUB, 128), lambda i: (i, 0, 0))
    return pl.pallas_call(
        turn_kernel,
        grid=(CHUNKS,),
        in_specs=[blk],
        out_specs=blk,
        out_shape=jax.ShapeDtypeStruct((BINS, SUB, 128), BF),
        compiler_params=VMEM,
        cost_estimate=pl.CostEstimate(flops=10**6, bytes_accessed=25 * 10**6, transcendentals=0),
        name="turn",
    )(own)


def corr_kernel(place, order, *refs):
    pieces = refs[:CHUNKS]
    own, rot = refs[CHUNKS : CHUNKS + 2], refs[CHUNKS + 2 : CHUNKS + 4]
    inv, table = refs[CHUNKS + 4 : CHUNKS + 6]
    outs = refs[CHUNKS + 6 : CHUNKS + 10]
    src, work, rows, sems = refs[CHUNKS + 10 :]
    step = pl.program_id(0)
    copies = [pltpu.make_async_copy(piece, src.at[m], sems.at[m]) for m, piece in enumerate(pieces)]

    @pl.when(step == 0)
    def _():
        for copy in copies:
            copy.start()

    for m, copy in enumerate(copies):
        @pl.when(step == m // 2)
        def _(copy=copy):
            copy.wait()

    zero = jnp.zeros((SUB, 128), BF)

    def diagonal(a, b):
        return jnp.concatenate(
            [jnp.concatenate([a, zero], axis=1), jnp.concatenate([zero, b], axis=1)], axis=0
        )

    for e in range(2):
        for k in range(0, KC, 2):
            x = src[2 * step + e, k : k + 2].reshape(2 * SUB, 128).T
            h = jnp.dot(x[:BLOCK], diagonal(own[e][k], own[e][k + 1]), preferred_element_type=F32)
            h += jnp.dot(x[BLOCK:], diagonal(rot[e][k], rot[e][k + 1]), preferred_element_type=F32)
            work[e * KC + k] = h[:, :128]
            work[e * KC + k + 1] = h[:, 128:]
    z = jnp.swapaxes(work[...], 0, 1)
    low = lax.broadcasted_iota(jnp.int32, (2 * KC, 128), 1) < BLOCK
    offs = [pl.multiple_of(place[2 * step + e] * KC, KC) for e in range(2)]
    for p in range(BLOCK // 2):
        u, v = z[2 * p], z[2 * p + 1]
        lanes = slice(p % 2 * 128, p % 2 * 128 + 128)
        re = jnp.where(low, u, pltpu.roll(v, 64, 1)).astype(BF)
        im = jnp.where(low, pltpu.roll(u, 64, 1), v).astype(BF)
        for e in range(2):
            rows[p // 2, pl.ds(offs[e], KC), lanes] = re[e * KC : e * KC + KC]
            rows[p // 2, pl.ds(offs[e] + BINS, KC), lanes] = im[e * KC : e * KC + KC]

    @pl.when(step == CHUNKS // 2 - 1)
    def _():
        for m in range(4):
            block = order[m]
            for q in range(4):
                y = jnp.dot(table[...], rows[4 * block + q], preferred_element_type=F32)
                cols = slice(q * 256, q * 256 + 256)
                outs[m][:, cols] = (y * inv[block, :, cols]).astype(BF)


def corr(place, order, pieces, own, rot, inv, table):
    here = [pl.BlockSpec((KC, SUB, 128), lambda i, p, o, e=e: (p[2 * i + e], 0, 0)) for e in range(2)]
    return pl.pallas_call(
        corr_kernel,
        grid_spec=pltpu.PrefetchScalarGridSpec(
            num_scalar_prefetch=2,
            grid=(CHUNKS // 2,),
            in_specs=[pl.BlockSpec(memory_space=pl.ANY)] * CHUNKS
            + here * 2
            + [
                pl.BlockSpec((4, 1, 1024), lambda i, p, o: (0, 0, 0)),
                pl.BlockSpec((LAGS, 2 * BINS), lambda i, p, o: (0, 0)),
            ],
            out_specs=[pl.BlockSpec((LAGS, 1024), lambda i, p, o: (0, 0))] * 4,
            scratch_shapes=[
                pltpu.VMEM((CHUNKS, KC, SUB, 128), BF),
                pltpu.VMEM((2 * KC, BLOCK, 128), F32),
                pltpu.VMEM((BLOCK // 4, 2 * BINS, 256), BF),
                pltpu.SemaphoreType.DMA((CHUNKS,)),
            ],
        ),
        out_shape=[jax.ShapeDtypeStruct((LAGS, 1024), BF)] * 4,
        compiler_params=VMEM,
        cost_estimate=pl.CostEstimate(flops=22 * 10**9, bytes_accessed=40 * 10**6, transcendentals=0),
        name="corr",
    )(place, order, *pieces, own, own, rot, rot, inv, table)


def finish_kernel(a, b, c, *refs):
    total = a[...].astype(F32) + b[...].astype(F32) + c[...].astype(F32)
    refs[-1][0] = total.T.astype(BF)


def finish(step, near, near_got, far_sum, base=None):
    cols = 512
    extra = [] if base is None else [base]
    return pl.pallas_call(
        finish_kernel,
        grid=(1024 // cols,),
        in_specs=[pl.BlockSpec((LAGS, cols), lambda j: (0, j))] * 3
        + [pl.BlockSpec(memory_space=pl.ANY)] * len(extra),
        out_specs=pl.BlockSpec((1, cols, LAGS), lambda j: (step, j, 0)),
        out_shape=jax.ShapeDtypeStruct((STEPS, 1024, LAGS), BF),
        input_output_aliases={3: 0} if extra else {},
        compiler_params=VMEM,
        name="finish",
    )(near, near_got, far_sum, *extra)


def lag_table():
    k = np.arange(1, BINS + 1)[None, :]
    tau = np.arange(LAGS)[:, None] - LAGS // 2
    ph = ((k * tau) % NFFT) * (2 * np.pi / NFFT)
    w = np.concatenate([np.cos(ph), -np.sin(ph)], axis=1) / math.sqrt(BINS)
    return jnp.asarray(w, BF)


def along_x(a, d):
    return lax.ppermute(a, "station", [(s, s - s % 4 + (s + d) % 4) for s in range(32)])


def along_z(a, d):
    return lax.ppermute(a, "station", [(s, (s + 8 * d) % 32) for s in range(32)])


def swap_y(a):
    return lax.ppermute(a, "station", [(s, s ^ 4) for s in range(32)])


def cut(a, index, size):
    return lax.dynamic_slice_in_dim(a, index * size, size, 0)


def pick(which, options):
    out = options[0]
    for n in range(1, 4):
        out = jnp.where(which == n, options[n], out)
    return out


def barrier(*arrays):
    return lax.optimization_barrier(arrays)


def spread(sends, shifts, work=None, args=()):
    n = len(sends)
    held = barrier(*sends, *args)
    got = [shift(a) for a, shift in zip(held[:n], shifts)]
    done = list(work(*held[n:])) if work else []
    return barrier(*got, *done)


HOPS = (2, 1, 3)
TO_X = {d: lambda a, d=d: along_x(a, d) for d in HOPS}
TO_Z = {d: lambda a, d=d: along_z(a, d) for d in HOPS}
X_THEN_Z = [to[d] for d in HOPS for to in (TO_X, TO_Z)]
Z_THEN_X = [to[d] for d in HOPS for to in (TO_Z, TO_X)]


def by_hop(got):
    return [[got[2 * HOPS.index(d) + n] for d in (1, 2, 3)] for n in range(2)]


def broadcast(own, ready, counts, roots, z, h, x):
    from_x, from_z = by_hop(spread(ready, X_THEN_Z))

    def own_a(q):
        return lambda ins, s: ins[0].at[pl.ds(s[4] * 64 + s[q] * 16, 16)]

    def own_b(q):
        return lambda ins, s: ins[0].at[pl.ds(s[5] * 64 + s[q] * 16, 16)]

    def came(n, q):
        return lambda ins, s: ins[n].at[pl.ds(s[q] * 16, 16)]

    def row(n):
        return lambda ins, s: ins[n].at[64:65]

    scalars = jnp.stack(
        [(x - r[2]) & 3 for r in roots]
        + [(z - r[0]) & 3 for r in roots]
        + [x, 4 + z]
        + [(z + d) & 3 for d in range(4)]
        + [(x + d) & 3 for d in range(4)]
    ).astype(jnp.int32)
    tasks = []
    for d in range(4):
        for i in range(STEPS):
            tasks += [
                (lambda outs, d=d, i=i: outs[d].at[i, :16], i, [own_a(6 + d)] + [came(n, 6 + d) for n in (2, 3, 4)]),
                (lambda outs, d=d, i=i: outs[d].at[i, 16:], i, [row(n) for n in (1, 2, 3, 4)]),
                (lambda outs, d=d, i=i: outs[4 + d].at[i], 2 + i, [own_b(10 + d)] + [came(n, 10 + d) for n in (5, 6, 7)]),
            ]
    shapes = [(STEPS, 17, SUB, 128)] * 4 + [(STEPS, 16, SUB, 128)] * 4
    cuts = choose(scalars, [own, ready[0], *from_x, *from_z], shapes, tasks)
    got = spread(
        cuts[1:4] + cuts[5:], [TO_Z[d] for d in (1, 2, 3)] + [TO_X[d] for d in (1, 2, 3)]
    )
    got_a = [cuts[0], *got[:3]]
    got_b = [cuts[4], *got[3:]]
    mine_a = jnp.stack([pick((z - r[0]) & 3, [g[i] for g in got_a]) for i, r in enumerate(roots)])
    mine_b = jnp.stack([pick((x - r[2]) & 3, [g[i] for g in got_b]) for i, r in enumerate(roots)])
    other_a, other_b = spread([mine_a, mine_b], [swap_y] * 2)
    here = [h == r[1] for r in roots]
    sub = [
        jnp.stack([jnp.where(here[i], mine[i, :16], other[i, :16]) for i in range(STEPS)])
        for mine, other in ((mine_a, other_a), (mine_b, other_b))
    ]

    def scales(mine, other):
        out = []
        for i in range(STEPS):
            src_counts = jnp.where(here[i], mine[i, 16, 0, :BLOCK], other[i, 16, 0, :BLOCK]).astype(F32)
            inv = 1.0 / jnp.minimum(src_counts[:, None], counts[None, :].astype(F32))
            out.append(inv.reshape(4, 1, 1024))
        return out

    got = spread(sub * 3, Z_THEN_X, scales, [mine_a, other_a])
    from_z, from_x = by_hop(got[:6])
    all_a = [sub[0], *from_z]
    all_b = [sub[1], *from_x]
    out = []
    for i in range(STEPS):
        a = jnp.concatenate([pick((z - q) & 3, [v[i] for v in all_a]) for q in range(4)])
        b = jnp.concatenate([pick((x - q) & 3, [v[i] for v in all_b]) for q in range(4)])
        out.append((a, b))
    return out, got[6:]


def other_core(a):
    return lax.ppermute(a, "tm", [(t, t ^ 1) for t in range(4)])


def other_chip(a):
    return lax.ppermute(a, "tm", [(t, t ^ 2) for t in range(4)])


def add(a, b):
    return (a.astype(F32) + b.astype(F32)).astype(BF)


def body(spectra, counts, block_ids):
    station, tm = lax.axis_index("station"), lax.axis_index("tm")
    z, h, x = station >> 3, station >> 2 & 1, station & 3

    def places(*list_of):
        return jnp.stack(list_of).astype(jnp.int32)

    ahead = places(*[v for d in HOPS for v in ((x + d) & 3, 4 + ((z + d) & 3))])
    own, *ready = whiten(ahead, spectra[0], counts)
    roots = [(block_ids[i] >> 3, block_ids[i] >> 2 & 1, block_ids[i] & 3) for i in range(STEPS)]
    ((a0, b0), (a1, b1)), (inv0, inv1) = broadcast(own, ready, counts[0], roots, z, h, x)

    place = places(
        *[(x + d) & 3 for d in (0, 3, 1, 2)], *[4 + ((z + d) & 3) for d in (0, 3, 1, 2)]
    )
    table = lag_table()
    order = places((tm ^ 2) ^ 1, tm ^ 2, tm ^ 1, tm)

    up, down = [TO_X[1], TO_Z[1]], [TO_X[3], TO_Z[3]]
    a0_up, b0_up, a0_down, b0_down, rot = spread(
        [a0, b0, a0, b0], up + down, lambda v: [turn(v)], [own]
    )
    a0_far, b0_far, a1_down, b1_down = spread([a0_up, b0_up, a1, b1], up + down)
    a1_up, b1_up, a1_far, b1_far, *lag0 = spread(
        [a1, b1, a1_down, b1_down],
        up + down,
        lambda *v: corr(place, order, v[:8], *v[8:], table),
        [a0, a0_up, a0_down, a0_far, b0, b0_up, b0_down, b0_far, own, rot, inv0],
    )
    (far_got,) = spread([lag0[0]], [other_core])
    far_sum0, near_got0, *lag1 = spread(
        [add(lag0[1], far_got), lag0[2]],
        [other_chip, other_core],
        lambda *v: corr(place, order, v[:8], *v[8:], table),
        [a1, a1_up, a1_down, a1_far, b1, b1_up, b1_down, b1_far, own, rot, inv1],
    )
    (far_got,) = spread([lag1[0]], [other_core])
    far_sum1, near_got1, out = spread(
        [add(lag1[1], far_got), lag1[2]],
        [other_chip, other_core],
        lambda *v: [finish(0, *v)],
        [lag0[3], near_got0, far_sum0],
    )
    out = finish(1, lag1[3], near_got1, far_sum1, out)
    return out.reshape(STEPS, 16, BLOCK, LAGS)


def solution(mesh):
    from jax.sharding import PartitionSpec as P

    return jax.shard_map(
        body,
        mesh=mesh,
        in_specs=(P("tm", None, "station", None), P("tm", "station"), P()),
        out_specs=P(None, "tm", "station", None),
        check_vma=False,
    )
```

```python
import math

import jax
import jax.numpy as jnp
import numpy as np
from jax import lax
from jax.experimental import pallas as pl
from jax.experimental.pallas import tpu as pltpu

NFFT, BINS, LAGS, BLOCK, STEPS, SUB = 2048, 512, 512, 64, 2, 48
EPS = 1e-6
F32, BF = jnp.float32, jnp.bfloat16
VMEM = pltpu.CompilerParams(vmem_limit_bytes=56 * 2**20)
SB = 16
KC = 64
CHUNKS = BINS // KC
HALF = BINS // 2


def whiten_kernel(place, spec, counts, *refs):
    own, pieces, work = refs[0], refs[1:-1], refs[-1]
    base = pl.program_id(0) * SB
    live = jnp.concatenate([counts[...]] * 2, axis=1)
    for s in range(SB):
        v = spec[s].astype(F32)
        power = jnp.mean(v * v, axis=-1, keepdims=True)
        n = v * lax.rsqrt(power + EPS)
        mask = (base + s < live).astype(F32)
        work[s] = jnp.concatenate([n[:, :BINS], n[:, BINS:]], axis=0).T * mask
    own[...] = jnp.swapaxes(work[...], 0, 1).astype(BF)
    for m, piece in enumerate(pieces):
        piece[:KC] = own[pl.ds(pl.multiple_of(place[m] * KC, KC), KC)]
        if m % 2 == 0:
            piece[KC] = jnp.broadcast_to(live.astype(F32), (SB, 128)).astype(BF)


def whiten(place, spectra, counts):
    n = place.shape[0]
    sizes = [KC + 1 - m % 2 for m in range(n)]
    return pl.pallas_call(
        whiten_kernel,
        grid_spec=pltpu.PrefetchScalarGridSpec(
            num_scalar_prefetch=1,
            grid=(SUB // SB,),
            in_specs=[
                pl.BlockSpec((SB, BLOCK, 2 * BINS), lambda i, p: (i, 0, 0)),
                pl.BlockSpec((1, BLOCK), lambda i, p: (0, 0)),
            ],
            out_specs=[pl.BlockSpec((BINS, SB, 128), lambda i, p: (0, i, 0))]
            + [pl.BlockSpec((size, SB, 128), lambda i, p: (0, i, 0)) for size in sizes],
            scratch_shapes=[pltpu.VMEM((SB, BINS, 128), F32)],
        ),
        out_shape=[jax.ShapeDtypeStruct((BINS, SUB, 128), BF)]
        + [jax.ShapeDtypeStruct((size, SUB, 128), BF) for size in sizes],
        compiler_params=VMEM,
        cost_estimate=pl.CostEstimate(flops=10**8, bytes_accessed=18 * 10**6, transcendentals=0),
        name="whiten",
    )(place, spectra, counts)


def choose(scalars, inputs, shapes, tasks):
    n = len(inputs)

    def kernel(*refs):
        s, ins, outs, sems = refs[0], refs[1 : 1 + n], refs[1 + n : -1], refs[-1]
        copies = []
        for m, (dst, which, sources) in enumerate(tasks):
            options = [pltpu.make_async_copy(src(ins, s), dst(outs), sems.at[m]) for src in sources]
            for number, copy in enumerate(options):
                @pl.when(s[which] == number)
                def _(copy=copy):
                    copy.start()
            copies.append(options[0])
        for copy in copies:
            copy.wait()

    anywhere = pl.BlockSpec(memory_space=pl.ANY)
    return pl.pallas_call(
        kernel,
        grid_spec=pltpu.PrefetchScalarGridSpec(
            num_scalar_prefetch=1,
            grid=(1,),
            in_specs=[anywhere] * n,
            out_specs=[pl.BlockSpec(shape, lambda i, s, n=len(shape): (0,) * n) for shape in shapes],
            scratch_shapes=[pltpu.SemaphoreType.DMA((len(tasks),))],
        ),
        out_shape=[jax.ShapeDtypeStruct(shape, BF) for shape in shapes],
        compiler_params=VMEM,
        cost_estimate=pl.CostEstimate(flops=10**6, bytes_accessed=6 * 10**6, transcendentals=0),
        name="choose",
    )(scalars, *inputs)


def turn_kernel(own, rot):
    v = own[...]
    rot[...] = jnp.concatenate([v[..., BLOCK:], -v[..., :BLOCK]], axis=-1)


def turn(own):
    blk = pl.BlockSpec((KC, SUB, 128), lambda i: (i, 0, 0))
    return pl.pallas_call(
        turn_kernel,
        grid=(CHUNKS,),
        in_specs=[blk],
        out_specs=blk,
        out_shape=jax.ShapeDtypeStruct((BINS, SUB, 128), BF),
        compiler_params=VMEM,
        cost_estimate=pl.CostEstimate(flops=10**6, bytes_accessed=25 * 10**6, transcendentals=0),
        name="turn",
    )(own)


def corr_kernel(place, order, *refs):
    pieces = refs[:CHUNKS]
    own, rot = refs[CHUNKS : CHUNKS + 2], refs[CHUNKS + 2 : CHUNKS + 4]
    inv, table = refs[CHUNKS + 4 : CHUNKS + 6]
    outs = refs[CHUNKS + 6 : CHUNKS + 10]
    src, work, rows, sems = refs[CHUNKS + 10 :]
    step = pl.program_id(0)
    copies = [pltpu.make_async_copy(piece, src.at[m], sems.at[m]) for m, piece in enumerate(pieces)]

    @pl.when(step == 0)
    def _():
        for copy in copies:
            copy.start()

    for m, copy in enumerate(copies):
        @pl.when(step == m // 2)
        def _(copy=copy):
            copy.wait()

    zero = jnp.zeros((SUB, 128), BF)

    def diagonal(a, b):
        return jnp.concatenate(
            [jnp.concatenate([a, zero], axis=1), jnp.concatenate([zero, b], axis=1)], axis=0
        )

    for e in range(2):
        for k in range(0, KC, 2):
            x = src[2 * step + e, k : k + 2].reshape(2 * SUB, 128).T
            h = jnp.dot(x[:BLOCK], diagonal(own[e][k], own[e][k + 1]), preferred_element_type=F32)
            h += jnp.dot(x[BLOCK:], diagonal(rot[e][k], rot[e][k + 1]), preferred_element_type=F32)
            work[e * KC + k] = h[:, :128]
            work[e * KC + k + 1] = h[:, 128:]
    z = jnp.swapaxes(work[...], 0, 1)
    low = lax.broadcasted_iota(jnp.int32, (2 * KC, 128), 1) < BLOCK
    offs = [pl.multiple_of(place[2 * step + e] * KC, KC) for e in range(2)]
    for p in range(BLOCK // 2):
        u, v = z[2 * p], z[2 * p + 1]
        lanes = slice(p % 2 * 128, p % 2 * 128 + 128)
        re = jnp.where(low, u, pltpu.roll(v, 64, 1)).astype(BF)
        im = jnp.where(low, pltpu.roll(u, 64, 1), v).astype(BF)
        for e in range(2):
            rows[p // 2, pl.ds(offs[e], KC), lanes] = re[e * KC : e * KC + KC]
            rows[p // 2, pl.ds(offs[e] + BINS, KC), lanes] = im[e * KC : e * KC + KC]

    @pl.when(step == CHUNKS // 2 - 1)
    def _():
        for m in range(4):
            block = order[m]
            for q in range(4):
                y = jnp.dot(table[...], rows[4 * block + q], preferred_element_type=F32)
                cols = slice(q * 256, q * 256 + 256)
                outs[m][:, cols] = (y * inv[block, :, cols]).astype(BF)


def corr(place, order, pieces, own, rot, inv, table):
    here = [pl.BlockSpec((KC, SUB, 128), lambda i, p, o, e=e: (p[2 * i + e], 0, 0)) for e in range(2)]
    return pl.pallas_call(
        corr_kernel,
        grid_spec=pltpu.PrefetchScalarGridSpec(
            num_scalar_prefetch=2,
            grid=(CHUNKS // 2,),
            in_specs=[pl.BlockSpec(memory_space=pl.ANY)] * CHUNKS
            + here * 2
            + [
                pl.BlockSpec((4, 1, 1024), lambda i, p, o: (0, 0, 0)),
                pl.BlockSpec((LAGS, 2 * BINS), lambda i, p, o: (0, 0)),
            ],
            out_specs=[pl.BlockSpec((LAGS, 1024), lambda i, p, o: (0, 0))] * 4,
            scratch_shapes=[
                pltpu.VMEM((CHUNKS, KC, SUB, 128), BF),
                pltpu.VMEM((2 * KC, BLOCK, 128), F32),
                pltpu.VMEM((BLOCK // 4, 2 * BINS, 256), BF),
                pltpu.SemaphoreType.DMA((CHUNKS,)),
            ],
        ),
        out_shape=[jax.ShapeDtypeStruct((LAGS, 1024), BF)] * 4,
        compiler_params=VMEM,
        cost_estimate=pl.CostEstimate(flops=22 * 10**9, bytes_accessed=40 * 10**6, transcendentals=0),
        name="corr",
    )(place, order, *pieces, own, own, rot, rot, inv, table)


def finish_kernel(a, b, c, *refs):
    total = a[...].astype(F32) + b[...].astype(F32) + c[...].astype(F32)
    refs[-1][0] = total.T.astype(BF)


def finish(step, near, near_got, far_sum, base=None):
    cols = 256
    extra = [] if base is None else [base]
    return pl.pallas_call(
        finish_kernel,
        grid=(1024 // cols,),
        in_specs=[pl.BlockSpec((LAGS, cols), lambda j: (0, j))] * 3
        + [pl.BlockSpec(memory_space=pl.ANY)] * len(extra),
        out_specs=pl.BlockSpec((1, cols, LAGS), lambda j: (step, j, 0)),
        out_shape=jax.ShapeDtypeStruct((STEPS, 1024, LAGS), BF),
        input_output_aliases={3: 0} if extra else {},
        compiler_params=VMEM,
        name="finish",
    )(near, near_got, far_sum, *extra)


def lag_table():
    k = np.arange(1, BINS + 1)[None, :]
    tau = np.arange(LAGS)[:, None] - LAGS // 2
    ph = ((k * tau) % NFFT) * (2 * np.pi / NFFT)
    w = np.concatenate([np.cos(ph), -np.sin(ph)], axis=1) / math.sqrt(BINS)
    return jnp.asarray(w, BF)


def along_x(a, d):
    return lax.ppermute(a, "station", [(s, s - s % 4 + (s + d) % 4) for s in range(32)])


def along_z(a, d):
    return lax.ppermute(a, "station", [(s, (s + 8 * d) % 32) for s in range(32)])


def swap_y(a):
    return lax.ppermute(a, "station", [(s, s ^ 4) for s in range(32)])


def cut(a, index, size):
    return lax.dynamic_slice_in_dim(a, index * size, size, 0)


def pick(which, options):
    out = options[0]
    for n in range(1, 4):
        out = jnp.where(which == n, options[n], out)
    return out


def barrier(*arrays):
    return lax.optimization_barrier(arrays)


def spread(sends, shifts, work=None, args=()):
    n = len(sends)
    held = barrier(*sends, *args)
    got = [shift(a) for a, shift in zip(held[:n], shifts)]
    done = list(work(*held[n:])) if work else []
    return barrier(*got, *done)


HOPS = (2, 1, 3)
TO_X = {d: lambda a, d=d: along_x(a, d) for d in HOPS}
TO_Z = {d: lambda a, d=d: along_z(a, d) for d in HOPS}
X_THEN_Z = [to[d] for d in HOPS for to in (TO_X, TO_Z)]
Z_THEN_X = [to[d] for d in HOPS for to in (TO_Z, TO_X)]


def by_hop(got):
    return [[got[2 * HOPS.index(d) + n] for d in (1, 2, 3)] for n in range(2)]


def broadcast(own, ready, counts, roots, z, h, x):
    from_x, from_z = by_hop(spread(ready, X_THEN_Z))

    def own_a(q):
        return lambda ins, s: ins[0].at[pl.ds(s[4] * 64 + s[q] * 16, 16)]

    def own_b(q):
        return lambda ins, s: ins[0].at[pl.ds(s[5] * 64 + s[q] * 16, 16)]

    def came(n, q):
        return lambda ins, s: ins[n].at[pl.ds(s[q] * 16, 16)]

    def row(n):
        return lambda ins, s: ins[n].at[64:65]

    scalars = jnp.stack(
        [(x - r[2]) & 3 for r in roots]
        + [(z - r[0]) & 3 for r in roots]
        + [x, 4 + z]
        + [(z + d) & 3 for d in range(4)]
        + [(x + d) & 3 for d in range(4)]
    ).astype(jnp.int32)
    tasks = []
    for d in range(4):
        for i in range(STEPS):
            tasks += [
                (lambda outs, d=d, i=i: outs[d].at[i, :16], i, [own_a(6 + d)] + [came(n, 6 + d) for n in (2, 3, 4)]),
                (lambda outs, d=d, i=i: outs[d].at[i, 16:], i, [row(n) for n in (1, 2, 3, 4)]),
                (lambda outs, d=d, i=i: outs[4 + d].at[i], 2 + i, [own_b(10 + d)] + [came(n, 10 + d) for n in (5, 6, 7)]),
            ]
    shapes = [(STEPS, 17, SUB, 128)] * 4 + [(STEPS, 16, SUB, 128)] * 4
    cuts = choose(scalars, [own, ready[0], *from_x, *from_z], shapes, tasks)
    got = spread(
        cuts[1:4] + cuts[5:], [TO_Z[d] for d in (1, 2, 3)] + [TO_X[d] for d in (1, 2, 3)]
    )
    got_a = [cuts[0], *got[:3]]
    got_b = [cuts[4], *got[3:]]
    mine_a = jnp.stack([pick((z - r[0]) & 3, [g[i] for g in got_a]) for i, r in enumerate(roots)])
    mine_b = jnp.stack([pick((x - r[2]) & 3, [g[i] for g in got_b]) for i, r in enumerate(roots)])
    other_a, other_b = spread([mine_a, mine_b], [swap_y] * 2)
    here = [h == r[1] for r in roots]
    sub = [
        jnp.stack([jnp.where(here[i], mine[i, :16], other[i, :16]) for i in range(STEPS)])
        for mine, other in ((mine_a, other_a), (mine_b, other_b))
    ]

    def scales(mine, other):
        out = []
        for i in range(STEPS):
            src_counts = jnp.where(here[i], mine[i, 16, 0, :BLOCK], other[i, 16, 0, :BLOCK]).astype(F32)
            inv = 1.0 / jnp.minimum(src_counts[:, None], counts[None, :].astype(F32))
            out.append(inv.reshape(4, 1, 1024))
        return out

    got = spread(sub * 3, Z_THEN_X, scales, [mine_a, other_a])
    from_z, from_x = by_hop(got[:6])
    all_a = [sub[0], *from_z]
    all_b = [sub[1], *from_x]
    out = []
    for i in range(STEPS):
        a = jnp.concatenate([pick((z - q) & 3, [v[i] for v in all_a]) for q in range(4)])
        b = jnp.concatenate([pick((x - q) & 3, [v[i] for v in all_b]) for q in range(4)])
        out.append((a, b))
    return out, got[6:]


def other_core(a):
    return lax.ppermute(a, "tm", [(t, t ^ 1) for t in range(4)])


def other_chip(a):
    return lax.ppermute(a, "tm", [(t, t ^ 2) for t in range(4)])


def add(a, b):
    return (a.astype(F32) + b.astype(F32)).astype(BF)


def body(spectra, counts, block_ids):
    station, tm = lax.axis_index("station"), lax.axis_index("tm")
    z, h, x = station >> 3, station >> 2 & 1, station & 3

    def places(*list_of):
        return jnp.stack(list_of).astype(jnp.int32)

    ahead = places(*[v for d in HOPS for v in ((x + d) & 3, 4 + ((z + d) & 3))])
    own, *ready = whiten(ahead, spectra[0], counts)
    roots = [(block_ids[i] >> 3, block_ids[i] >> 2 & 1, block_ids[i] & 3) for i in range(STEPS)]
    ((a0, b0), (a1, b1)), (inv0, inv1) = broadcast(own, ready, counts[0], roots, z, h, x)

    place = places(
        *[(x + d) & 3 for d in (0, 3, 1, 2)], *[4 + ((z + d) & 3) for d in (0, 3, 1, 2)]
    )
    table = lag_table()
    order = places((tm ^ 2) ^ 1, tm ^ 2, tm ^ 1, tm)

    up, down = [TO_X[1], TO_Z[1]], [TO_X[3], TO_Z[3]]
    a0_up, b0_up, a0_down, b0_down, rot = spread(
        [a0, b0, a0, b0], up + down, lambda v: [turn(v)], [own]
    )
    a0_far, b0_far, a1_down, b1_down = spread([a0_up, b0_up, a1, b1], up + down)
    a1_up, b1_up, a1_far, b1_far, *lag0 = spread(
        [a1, b1, a1_down, b1_down],
        up + down,
        lambda *v: corr(place, order, v[:8], *v[8:], table),
        [a0, a0_up, a0_down, a0_far, b0, b0_up, b0_down, b0_far, own, rot, inv0],
    )
    (far_got,) = spread([lag0[0]], [other_core])
    far_sum0, near_got0, *lag1 = spread(
        [add(lag0[1], far_got), lag0[2]],
        [other_chip, other_core],
        lambda *v: corr(place, order, v[:8], *v[8:], table),
        [a1, a1_up, a1_down, a1_far, b1, b1_up, b1_down, b1_far, own, rot, inv1],
    )
    (far_got,) = spread([lag1[0]], [other_core])
    far_sum1, near_got1, out = spread(
        [add(lag1[1], far_got), lag1[2]],
        [other_chip, other_core],
        lambda *v: [finish(0, *v)],
        [lag0[3], near_got0, far_sum0],
    )
    out = finish(1, lag1[3], near_got1, far_sum1, out)
    return out.reshape(STEPS, 16, BLOCK, LAGS)


def solution(mesh):
    from jax.sharding import PartitionSpec as P

    return jax.shard_map(
        body,
        mesh=mesh,
        in_specs=(P("tm", None, "station", None), P("tm", "station"), P()),
        out_specs=P(None, "tm", "station", None),
        check_vma=False,
    )
```
